128 devices in a mesh: space: 16 (over z, x), occ: 8 (over y, core).
Axes of the slice: x: 4, y: 4, z: 4, core: 2. Of those that a mesh axis runs over, the one named last changes fastest.
Arguments:
- factors: bfloat16 [48, 512, 8192], P('space', None, 'occ'), may hold values from -1.5 to 1.5
- pair_mask: int32 [48, 4], P('space'), may hold values from 0 to 1, as said below
Outputs:
- forward_k: float32 [48, 4, 512, 512], P('space', None, None, 'occ')
- backward_k: float32 [48, 4, 512, 512], P('space', None, 'occ')
The draws below stay inside these ranges and needn't reach their ends.
Inputs may be any that keep to these rules, and one draw needn't show every extreme that they name: pair_mask[A, s] is 1 where the block pair (A, A + 1 + s) passed screening and 0 otherwise; it is 0 wherever A + 1 + s >= 48.
All inputs are finite; a program needn't handle non-finite values.
Results may differ from the reference program's by a relative error of at most 0.0003.
Values may be sent and summed in bfloat16 or wider, within the bound.
No kernel may reach another device: no remote copies, remote signals or barrier semaphores. Data moves between devices by JAX's collectives and lax.ppermute only.
A program may use at most 128 MiB of HBM per device.

```python
import jax
import jax.numpy as jnp
from jax import lax

BF = 512
AUX = 16
OCC = 64
REACH = 4
NBLK = 48
COLS = 8192
N_OCC = 8


def draw_pair_mask(key, part):
    key = jax.random.fold_in(key, 7)
    first, second = jax.random.split(key)
    density = jax.random.randint(first, (NBLK, 1), 1, 9)
    levels = density * density // 8
    trials = jax.random.randint(second, (NBLK, REACH), 0, 8)
    partner = jnp.arange(NBLK)[:, None] + 1 + jnp.arange(REACH)[None, :]
    return jnp.where((trials < levels) & (partner < NBLK), 1, 0).astype(jnp.int32)


def steps_of(own_key, dims, cuts, low, top_value):
    gain = 1.0
    for dim, blocks in cuts:
        draws = jax.random.uniform(jax.random.fold_in(jax.random.fold_in(own_key, 6), dim), (blocks,), jnp.float32, low / len(cuts), top_value / len(cuts))
        gain = gain * jnp.repeat(jnp.exp(draws), dims[dim] // blocks).reshape((-1,) + (1,) * (len(dims) - 1 - dim))
    return gain


def centred(key, extent, scale, reach, pieces=(), kind=jnp.bfloat16):
    loudness = steps_of(key, extent, pieces, -0.22, 0.18) if pieces else 1.0
    array = jax.random.normal(key, extent, jnp.float32) * scale * loudness
    return jnp.minimum(jnp.maximum(array, -reach), reach).astype(kind)


def setup_inputs(seed: int = 0) -> dict:
    key_list = jax.random.split(jax.random.key(seed), 3)
    return {
        "factors": centred(key_list[0], (NBLK, BF, COLS), ((AUX * OCC * N_OCC) ** -0.25), 1.5, ((0, 16), (2, 8))),
        "pair_mask": draw_pair_mask(jax.random.fold_in(key_list[2], 71), 0),
    }


def reference(factors, pair_mask):
    width = AUX * OCC

    def one_block(index):
        left = lax.dynamic_index_in_dim(factors, index, 0, False).astype(jnp.float32)
        left = left.reshape(BF, N_OCC, width)
        tiles = []
        for slot in range(REACH):
            other = jnp.minimum(index + 1 + slot, NBLK - 1).astype(jnp.int32)
            right = lax.dynamic_index_in_dim(factors, other, 0, False).astype(jnp.float32)
            right = right.reshape(BF, N_OCC, width)
            parts = jnp.einsum("bjk,cjk->jbc", left, right, precision=lax.Precision.HIGHEST)
            weight = pair_mask[index, slot].astype(jnp.float32)
            tiles.append(jnp.sum(parts * weight, axis=0))
        return jnp.stack(tiles, 0)

    forward = lax.map(one_block, jnp.arange(NBLK, dtype=jnp.int32))
    backs = []
    for slot in range(REACH):
        moved = jnp.concatenate([jnp.zeros((1 + slot, BF, BF), jnp.float32), forward[: NBLK - 1 - slot, slot]], 0)
        backs.append(jnp.swapaxes(moved, 1, 2))
    backward = jnp.stack(backs, 1)
    return forward, backward
```

```python
import functools

import jax
import jax.numpy as jnp
from jax import lax
from jax.experimental import pallas as pl
from jax.experimental.pallas import tpu as pltpu
from jax.sharding import PartitionSpec as P

BF = 512
HALF = 256
SLICE = 64
CHIPS = 4
STEPS = 256.0
TOP = 32700.0
LN2 = 0.6931471805599453


def space_pairs(by):
    return [(i, i + by) for i in range(16) if 0 <= i + by < 16]


SIBLING = [(o, o ^ 1) for o in range(8)]
SAME_CORE = [[0, 2, 4, 6], [1, 3, 5, 7]]


def barrier(*values):
    return lax.optimization_barrier(values)


def half_rows(ref, index, core):
    return jnp.concatenate(
        [ref[index, pl.ds((2 * y + core) * SLICE, SLICE), :] for y in range(CHIPS)], 0
    )


def code(acc):
    parts = [acc[y * SLICE : (y + 1) * SLICE] for y in range(CHIPS)]
    tops = jnp.concatenate([jnp.max(jnp.abs(part), 0, keepdims=True) for part in parts], 0)
    level = jnp.ceil(jnp.log(jnp.maximum(tops, 1e-30) / TOP) * (STEPS / LN2))
    gain = jnp.exp(level * (-LN2 / STEPS))
    coded = [
        jnp.round(part * gain[y : y + 1]).astype(jnp.int32).astype(jnp.int16)
        for y, part in enumerate(parts)
    ]
    return coded, level.astype(jnp.int32)


def pair_kernel(pairs, names, core_ref, *refs):
    ins, (out_ref, *extra) = refs[: len(names)], refs[len(names) :]
    core = core_ref[0]
    by_name = dict(zip(names, ins))
    levels = []

    def left(name, index, other):
        return by_name[name + ("_sib" if other else "_own")][index]

    def right(name, index, other):
        if name == "half":
            return by_name["half"][int(other)]
        return half_rows(by_name[name + ("_sib" if other else "_own")], index, core)

    for p, (a, b) in enumerate(pairs):
        acc = None
        for other in (False, True):
            term = lax.dot_general(
                right(*b, other),
                left(*a, other),
                (((1,), (1,)), ((), ())),
                preferred_element_type=jnp.float32,
            )
            acc = term if acc is None else acc + term
        coded, level = code(acc)
        for y in range(CHIPS):
            out_ref[y, p * SLICE : (p + 1) * SLICE, :] = coded[y]
        levels.append(level)
    n = len(pairs)
    for y in range(CHIPS):
        rows = [level[y : y + 1] for level in levels]
        rows.append(jnp.zeros((16 - n, BF), jnp.int32))
        out_ref[y, n * SLICE : n * SLICE + 16, :] = jnp.concatenate(rows, 0).astype(jnp.int16)
    if extra:
        for other in (False, True):
            extra[0][int(other)] = right("mine", 1, other)


def pair_products(core, pairs, operands, with_half=False):
    names = list(operands)
    n = len(pairs)
    shapes = [jax.ShapeDtypeStruct((CHIPS, n * SLICE + 16, BF), jnp.int16)]
    if with_half:
        shapes.append(jax.ShapeDtypeStruct((2, HALF, 1024), jnp.bfloat16))
    out = pl.pallas_call(
        functools.partial(pair_kernel, pairs, names),
        out_shape=shapes,
        in_specs=[pl.BlockSpec(memory_space=pltpu.SMEM)]
        + [pl.BlockSpec(memory_space=pltpu.VMEM)] * len(names),
        out_specs=[pl.BlockSpec(memory_space=pltpu.VMEM)] * len(shapes),
        compiler_params=pltpu.CompilerParams(vmem_limit_bytes=40 << 20),
        cost_estimate=pl.CostEstimate(
            flops=n * 2 * HALF * BF * 2048, bytes_accessed=8 << 20, transcendentals=0
        ),
    )(core, *operands.values())
    return out if with_half else out[0]


def add_kernel(masks, got_ref, mask_ref, before_ref, *outs):
    n = len(masks)
    scales = [
        jnp.exp(got_ref[y, n * SLICE : n * SLICE + 16, :].astype(jnp.float32) * (LN2 / STEPS))
        for y in range(CHIPS)
    ]
    for p, ((before, block, slot), places) in enumerate(masks):
        total = None
        for y in range(CHIPS):
            part = got_ref[y, p * SLICE : (p + 1) * SLICE, :].astype(jnp.float32)
            part = part * scales[y][p : p + 1]
            total = part if total is None else total + part
        weight = (before_ref if before else mask_ref)[block, slot].astype(jnp.float32)
        total = total * weight
        for which, index in places:
            outs[which][index] = total


def add_parts(got, mask, before, masks, counts):
    return pl.pallas_call(
        functools.partial(add_kernel, masks),
        out_shape=[jax.ShapeDtypeStruct((k, SLICE, BF), jnp.float32) for k in counts],
        in_specs=[
            pl.BlockSpec(memory_space=pltpu.VMEM),
            pl.BlockSpec(memory_space=pltpu.SMEM),
            pl.BlockSpec(memory_space=pltpu.SMEM),
        ],
        out_specs=[pl.BlockSpec(memory_space=pltpu.VMEM)] * len(counts),
        compiler_params=pltpu.CompilerParams(vmem_limit_bytes=40 << 20),
        cost_estimate=pl.CostEstimate(flops=1 << 20, bytes_accessed=4 << 20, transcendentals=0),
    )(got, mask, before)


def finish_kernel(forward, backward, *refs):
    ins, (f_ref, b_ref) = refs[:-2], refs[-2:]
    for block in range(3):
        for slot in range(4):
            which, index = forward[block][slot]
            f_ref[block, slot] = ins[which][index].T
            which, index = backward[block][slot]
            b_ref[block, slot] = ins[which][index]


def finish(forward, backward, arrays):
    return pl.pallas_call(
        functools.partial(finish_kernel, forward, backward),
        out_shape=[
            jax.ShapeDtypeStruct((3, 4, BF, SLICE), jnp.float32),
            jax.ShapeDtypeStruct((3, 4, SLICE, BF), jnp.float32),
        ],
        in_specs=[pl.BlockSpec(memory_space=pltpu.VMEM)] * len(arrays),
        out_specs=[pl.BlockSpec(memory_space=pltpu.VMEM)] * 2,
        compiler_params=pltpu.CompilerParams(vmem_limit_bytes=40 << 20),
    )(*arrays)


def swap(value):
    return lax.ppermute(value, "occ", SIBLING)


def across(value):
    return lax.all_to_all(value, "occ", 0, 0, axis_index_groups=SAME_CORE)


def up(value):
    return lax.ppermute(value, "space", space_pairs(1))


def down(value):
    return lax.ppermute(value, "space", space_pairs(-1))


def on_device(own, mask):
    core = (lax.axis_index("occ") % 2).astype(jnp.int32).reshape(1)
    low = up(own[2:3])
    high = down(own[0:1])
    before = up(mask)
    own_sib = swap(own)
    mine = {"mine_own": own, "mine_sib": own_sib}
    M0, M1, M2 = ("mine", 0), ("mine", 1), ("mine", 2)
    coded0, half1 = pair_products(core, [(M0, M1), (M0, M2), (M1, M2)], mine, True)
    got0 = across(coded0)
    low, high, half1, middle = barrier(low, high, half1, own[1:2])
    low2 = up(middle)
    high2 = down(half1)
    low_sib, high_sib = swap((low, high))
    L, H = ("low", 0), ("high", 0)
    coded1 = pair_products(
        core,
        [(M0, H), (M1, H), (L, M0), (L, M1), (L, M2), (L, H)],
        mine | {"low_own": low, "low_sib": low_sib, "high_own": high, "high_sib": high_sib},
    )
    (sum0,) = add_parts(
        got0, mask, before, [((0, 0, 0), [(0, 0)]), ((0, 0, 1), [(0, 1)]), ((0, 1, 0), [(0, 2)])], [3]
    )
    got1 = across(coded1)
    low2_sib = swap(low2)
    coded2 = pair_products(
        core,
        [(M0, ("half", 0)), (M1, ("half", 0)), (L, M2)],
        mine | {"low_own": low2, "low_sib": low2_sib, "half": high2},
    )
    sum1, up1, down1 = add_parts(
        got1,
        mask,
        before,
        [
            ((0, 0, 2), [(0, 0), (1, 0)]),
            ((0, 1, 1), [(0, 1), (1, 1)]),
            ((1, 2, 0), [(0, 2), (2, 0)]),
            ((1, 2, 1), [(0, 3), (2, 1)]),
            ((1, 2, 2), [(0, 4), (2, 2)]),
            ((1, 2, 3), [(1, 2), (2, 3)]),
        ],
        [5, 3, 4],
    )
    below1 = up(up1)
    above1 = down(down1)
    got2 = across(coded2)
    sum2, up2, down2 = add_parts(
        got2,
        mask,
        before,
        [
            ((0, 0, 3), [(0, 0), (1, 0)]),
            ((0, 1, 2), [(0, 1), (1, 1)]),
            ((1, 1, 3), [(0, 2), (2, 0)]),
        ],
        [3, 2, 1],
    )
    below2 = up(up2)
    above2 = down(down2)
    S0, S1, S2, U1, D1, U2, D2 = range(7)
    forward = [
        [(S0, 0), (S0, 1), (S1, 0), (S2, 0)],
        [(S0, 2), (S1, 1), (S2, 1), (D2, 0)],
        [(D1, 0), (D1, 1), (D1, 2), (D1, 3)],
    ]
    backward = [
        [(S1, 2), (U1, 1), (U1, 0), (U1, 2)],
        [(S0, 0), (S1, 3), (U2, 1), (U2, 0)],
        [(S0, 2), (S0, 1), (S1, 4), (S2, 2)],
    ]
    return tuple(finish(forward, backward, [sum0, sum1, sum2, below1, above1, below2, above2]))


def solution(mesh):
    in_specs = (P("space", None, "occ"), P("space", None))
    out_specs = (P("space", None, None, "occ"), P("space", None, "occ", None))
    return jax.shard_map(
        on_device, mesh=mesh, in_specs=in_specs, out_specs=out_specs, check_vma=False
    )
```

```python
import functools

import jax
import jax.numpy as jnp
from jax import lax
from jax.experimental import pallas as pl
from jax.experimental.pallas import tpu as pltpu
from jax.sharding import PartitionSpec as P

BF = 512
COLS = 1024
HALF = 256
SLICE = 64
CHIPS = 4
STEPS = 256.0
TOP = 32700.0
LN2 = 0.6931471805599453

VMEM = pl.BlockSpec(memory_space=pltpu.VMEM)
SMEM = pl.BlockSpec(memory_space=pltpu.SMEM)
HBM = pl.BlockSpec(memory_space=pltpu.HBM)
PARAMS = pltpu.CompilerParams(vmem_limit_bytes=18 << 20)
OUTS = [jax.ShapeDtypeStruct((3, 4, SLICE, BF), jnp.float32)] * 2


def coded_rows(count):
    return count * SLICE + 16


def code(values):
    tops = jnp.concatenate([jnp.max(jnp.abs(v), 0, keepdims=True) for v in values], 0)
    level = jnp.ceil(jnp.log(jnp.maximum(tops, 1e-30) / TOP) * (STEPS / LN2))
    gain = jnp.exp(level * (-LN2 / STEPS))
    coded = [
        jnp.round(v * gain[i : i + 1]).astype(jnp.int32).astype(jnp.int16)
        for i, v in enumerate(values)
    ]
    return coded, level.astype(jnp.int32)


def level_rows(levels):
    rows = list(levels) + [jnp.zeros((16 - len(levels), BF), jnp.int32)]
    return jnp.concatenate(rows, 0).astype(jnp.int16)


def scales_of(rows):
    return jnp.exp(rows.astype(jnp.float32) * (LN2 / STEPS))


def pair_kernel(pairs, blocks, halved, names, together, lines, place_ref, *refs):
    ins = dict(zip(names, refs))
    outs = refs[len(names) :]
    if lines:
        outs, lines_ref = outs[:-1], outs[-1]
        lines_ref[...] = ins[lines][0, HALF : HALF + 16, :BF].astype(jnp.float32)
    if together:
        outs = [outs[0].at[d] for d in range(CHIPS)]
    core, chip = place_ref[0], place_ref[1]
    order = [d if together else (chip + d) % CHIPS for d in range(CHIPS)]

    def read(piece, start, rows):
        name, index = piece
        return ins[name][index, pl.ds(start, rows), :]

    def slices(pieces):
        rows = []
        for o in order:
            if len(pieces) == 2:
                start = (2 * (o % 2) + core) * SLICE
                low, high = (read(piece, start, SLICE) for piece in pieces)
                rows.append(jnp.where(o < 2, low, high))
            elif ins[pieces[0][0]].shape[1] == HALF:
                rows.append(read(pieces[0], o * SLICE, SLICE))
            else:
                rows.append(read(pieces[0], (2 * o + core) * SLICE, SLICE))
        return jnp.concatenate(rows, 0)

    def both_slices(pieces):
        rows = [read(pieces[0], o * 2 * SLICE, 2 * SLICE) for o in order]
        return jnp.concatenate(rows, 0)

    levels = []
    for p, (a, b) in enumerate(pairs):
        acc = None
        shared = a in halved
        for part in range(2):
            right = (both_slices if shared else slices)(blocks[b][part])
            pieces = blocks[a][part]
            rows = (HALF if shared else BF) // len(pieces)
            term = [
                lax.dot_general(
                    right,
                    read(piece, 0, rows),
                    (((1,), (1,)), ((), ())),
                    preferred_element_type=jnp.float32,
                )
                for piece in pieces
            ]
            term = jnp.concatenate(term, 1)
            acc = term if acc is None else acc + term
        if shared:
            parts = [
                jnp.concatenate(
                    [acc[k * SLICE : (k + 1) * SLICE] for k in (2 * d, 2 * d + 1)], 1
                )
                for d in range(CHIPS)
            ]
        else:
            parts = [acc[d * SLICE : (d + 1) * SLICE] for d in range(CHIPS)]
        coded, level = code(parts)
        for d in range(CHIPS):
            outs[d][p * SLICE : (p + 1) * SLICE, :] = coded[d]
        levels.append(level)
    end = len(pairs) * SLICE
    for d in range(CHIPS):
        outs[d][end : end + 16, :] = level_rows([v[d : d + 1] for v in levels])


def pair_products(place, pairs, blocks, operands, halved=(), together=False, lines=None):
    names = list(operands)
    n = len(pairs)
    rows = coded_rows(n)
    shapes = [jax.ShapeDtypeStruct((rows, BF), jnp.int16)] * CHIPS
    if together:
        shapes = [jax.ShapeDtypeStruct((CHIPS, rows, BF), jnp.int16)]
    if lines:
        shapes.append(jax.ShapeDtypeStruct((16, BF), jnp.float32))
    return pl.pallas_call(
        functools.partial(pair_kernel, pairs, blocks, halved, names, together, lines),
        out_shape=shapes,
        in_specs=[SMEM] + [VMEM] * len(names),
        out_specs=[VMEM] * len(shapes),
        compiler_params=PARAMS,
        cost_estimate=pl.CostEstimate(flops=1 << 20, bytes_accessed=1 << 16, transcendentals=0),
    )(place, *operands.values())


def pieces_kernel(place_ref, low_ref, high_ref, low_a_ref, low_b_ref, other_ref):
    low_a_ref[0] = low_ref[0, :HALF, :]
    low_b_ref[0] = low_ref[0, HALF:, :]
    core = 1 - place_ref[0]
    for y in range(CHIPS):
        start = (2 * y + core) * SLICE
        other_ref[0, y * SLICE : (y + 1) * SLICE, :] = high_ref[0, pl.ds(start, SLICE), :]


def pieces_for_sibling(place, low, high):
    return pl.pallas_call(
        pieces_kernel,
        out_shape=[jax.ShapeDtypeStruct((1, HALF, COLS), jnp.bfloat16)] * 3,
        in_specs=[SMEM, VMEM, VMEM],
        out_specs=[VMEM] * 3,
        compiler_params=PARAMS,
        cost_estimate=pl.CostEstimate(flops=1 << 10, bytes_accessed=1 << 10, transcendentals=0),
    )(place, low, high)


def second_kernel(place_ref, mask_ref, own_ref, sib_ref, up_ref, down_ref):
    core = place_ref[0]
    lines = [
        jnp.full((1, COLS), mask_ref[k // 4, k % 4].astype(jnp.float32), jnp.float32)
        for k in range(12)
    ]
    lines.append(jnp.zeros((4, COLS), jnp.float32))
    lines = jnp.concatenate(lines, 0).astype(jnp.bfloat16)
    for i, source in enumerate((own_ref, sib_ref)):
        up_ref[i, :HALF, :] = source[1, pl.ds(core * HALF, HALF), :]
        up_ref[i, HALF:, :] = lines
        for y in range(CHIPS):
            down_ref[i, y * SLICE : (y + 1) * SLICE, :] = source[
                1, pl.ds((2 * y + core) * SLICE, SLICE), :
            ]


def second_factors(place, mask, own, sib):
    return pl.pallas_call(
        second_kernel,
        out_shape=[
            jax.ShapeDtypeStruct((2, HALF + 16, COLS), jnp.bfloat16),
            jax.ShapeDtypeStruct((2, HALF, COLS), jnp.bfloat16),
        ],
        in_specs=[SMEM, SMEM, VMEM, VMEM],
        out_specs=[VMEM] * 2,
        compiler_params=PARAMS,
        cost_estimate=pl.CostEstimate(flops=1 << 10, bytes_accessed=1 << 10, transcendentals=0),
    )(place, mask, own, sib)


def add_kernel(places, first, sizes, halves, n_gots, lined, place_ref, *refs):
    gots, refs = refs[:n_gots], refs[n_gots:]
    if n_gots == 1:
        gots = [gots[0].at[d] for d in range(CHIPS)]
    mask_ref, refs = refs[0], refs[1:]
    if lined:
        lines_ref, refs = refs[0], refs[1:]
    if not first:
        refs = refs[2:]
    (f_ref, b_ref), refs = refs[:2], refs[2:]
    messages, refs = refs[: len(sizes)], refs[len(sizes) :]
    if halves:
        (same_ref, cross_ref, kept_ref, swap_ref), refs = refs[:4], refs[4:]
    sums, sems = refs
    levels = [[None] * size for size in sizes]
    writes = []
    n = len(places)
    scales = [scales_of(gots[d][n * SLICE : n * SLICE + 16, :]) for d in range(CHIPS)]
    for p, ((theirs, block, slot), goals) in enumerate(places):
        total = None
        for d in range(CHIPS):
            part = gots[d][p * SLICE : (p + 1) * SLICE, :].astype(jnp.float32)
            part = part * scales[d][p : p + 1]
            total = part if total is None else total + part
        if theirs:
            line = lines_ref[block * 4 + slot : block * 4 + slot + 1, :]
            total = total * line
        else:
            total = total * mask_ref[block, slot].astype(jnp.float32)
        coded = None
        for kind, *goal in goals:
            if kind == "m":
                which, index = goal
                if coded is None:
                    (coded,), level = code([total])
                levels[which][index] = level
                messages[which][index * SLICE : (index + 1) * SLICE, :] = coded
            elif kind == "halves":
                first_core = place_ref[0] == 0
                low, high = total[:, :HALF], total[:, HALF:]
                kept = jnp.where(first_core, low, high)
                other = jnp.where(first_core, high, low)
                kept_ref[...] = kept
                swap_ref[...] = other
                for ref, half in ((same_ref, kept), (cross_ref, other)):
                    (coded_half,), level = code([half])
                    ref[:SLICE, :] = coded_half
                    zeros = jnp.zeros((15, HALF), jnp.int32)
                    ref[SLICE:, :] = jnp.concatenate([level, zeros], 0).astype(jnp.int16)
            else:
                sums[p] = total
                writes.append((p, (f_ref if kind == "f" else b_ref).at[goal[0], goal[1]]))
    for m, size in enumerate(sizes):
        messages[m][size * SLICE : size * SLICE + 16, :] = level_rows(levels[m])
    writes = [
        pltpu.make_async_copy(sums.at[p], target, sems.at[k])
        for k, (p, target) in enumerate(writes)
    ]
    for copy in writes:
        copy.start()
    for copy in writes:
        copy.wait()


def add_parts(place, gots, masks, outs, places, sizes=(), halves=False):
    n = len(places)
    first = outs is None
    earlier = [] if first else list(outs)
    at = 1 + len(gots) + len(masks)
    shapes = OUTS + [jax.ShapeDtypeStruct((coded_rows(k), BF), jnp.int16) for k in sizes]
    if halves:
        shapes += [jax.ShapeDtypeStruct((SLICE + 16, HALF), jnp.int16)] * 2
        shapes += [jax.ShapeDtypeStruct((SLICE, HALF), jnp.float32)] * 2
    return pl.pallas_call(
        functools.partial(add_kernel, places, first, sizes, halves, len(gots), len(masks) > 1),
        out_shape=shapes,
        in_specs=[SMEM] + [VMEM] * len(gots) + [SMEM, VMEM][: len(masks)] + [HBM] * len(earlier),
        out_specs=[HBM] * 2 + [VMEM] * (len(shapes) - 2),
        scratch_shapes=[
            pltpu.VMEM((n, SLICE, BF), jnp.float32),
            pltpu.SemaphoreType.DMA((2 * n,)),
        ],
        input_output_aliases={} if first else {at: 0, at + 1: 1},
        compiler_params=PARAMS,
        cost_estimate=pl.CostEstimate(flops=1 << 20, bytes_accessed=1 << 16, transcendentals=0),
    )(place, *gots, *masks, *earlier)


def place_kernel(places, pair_places, place_ref, *refs):
    n, n_pairs = len(places), len(pair_places)
    messages, refs = refs[:n], refs[n:]
    halves, refs = refs[: 2 * n_pairs], refs[2 * n_pairs :]
    f_ref, b_ref, sums, sems = refs[2:]
    results = []
    for m, goals in enumerate(places):
        size = len(goals)
        scales = scales_of(messages[m][size * SLICE : size * SLICE + 16, :])
        for p, goal in enumerate(goals):
            part = messages[m][p * SLICE : (p + 1) * SLICE, :].astype(jnp.float32)
            results.append((part * scales[p : p + 1], goal))
    for m, goal in enumerate(pair_places):
        parts = []
        for half in halves[2 * m : 2 * m + 2]:
            part = half[:SLICE, :].astype(jnp.float32)
            if half.dtype == jnp.int16:
                part = part * scales_of(half[SLICE : SLICE + 16, :])[:1]
            parts.append(part)
        first_core = place_ref[0] == 0
        low = jnp.where(first_core, parts[0], parts[1])
        high = jnp.where(first_core, parts[1], parts[0])
        results.append((jnp.concatenate([low, high], 1), goal))
    writes = []
    for k, (value, (kind, block, slot)) in enumerate(results):
        sums[k] = value
        target = (f_ref if kind == "f" else b_ref).at[block, slot]
        writes.append(pltpu.make_async_copy(sums.at[k], target, sems.at[k]))
    for copy in writes:
        copy.start()
    for copy in writes:
        copy.wait()


def place_results(place, messages, halves, outs, places, pair_places=()):
    ins = list(messages) + list(halves)
    total = sum(map(len, places)) + len(pair_places)
    return pl.pallas_call(
        functools.partial(place_kernel, places, pair_places),
        out_shape=OUTS,
        in_specs=[SMEM] + [VMEM] * len(ins) + [HBM] * 2,
        out_specs=[HBM] * 2,
        scratch_shapes=[
            pltpu.VMEM((total, SLICE, BF), jnp.float32),
            pltpu.SemaphoreType.DMA((total,)),
        ],
        input_output_aliases={1 + len(ins): 0, 2 + len(ins): 1},
        compiler_params=PARAMS,
        cost_estimate=pl.CostEstimate(flops=1 << 20, bytes_accessed=1 << 16, transcendentals=0),
    )(place, *ins, *outs)


def swap(value):
    return lax.ppermute(value, "occ", [(o, o ^ 1) for o in range(2 * CHIPS)])


def chips_on(value, by):
    pairs = [
        (2 * y + core, 2 * ((y + by) % CHIPS) + core) for y in range(CHIPS) for core in range(2)
    ]
    return lax.ppermute(value, "occ", pairs)


def across(value):
    groups = [[2 * y + core for y in range(CHIPS)] for core in range(2)]
    return lax.all_to_all(value, "occ", 0, 0, axis_index_groups=groups)


def to_chips(parts):
    return [parts[0]] + [chips_on(parts[d], d) for d in range(1, CHIPS)]


def along_space(value, by):
    size = lax.axis_size("space")
    return lax.ppermute(value, "space", [(i, i + by) for i in range(size) if 0 <= i + by < size])


def up(value):
    return along_space(value, 1)


def down(value):
    return along_space(value, -1)


def down_across(value):
    groups, members = lax.axis_size("space"), 2 * CHIPS
    pairs = [
        (g * members + o, (g - 1) * members + (o ^ 1)) for g in range(1, groups) for o in range(members)
    ]
    return lax.ppermute(value, ("space", "occ"), pairs)


def on_device(own, mask):
    index = lax.axis_index("occ")
    place = jnp.stack([index % 2, index // 2]).astype(jnp.int32)
    own_sib = swap(own)
    low = own[2:3]
    low, own_after = lax.optimization_barrier((low, own))
    high = own_after[0:1]
    low, high = up(low), down(high)
    mine = {"own": own, "sib": own_sib}
    blocks = {k: ([("own", k)], [("sib", k)]) for k in range(3)}
    low2, high2 = second_factors(place, mask, own, own_sib)
    low2, high2 = up(low2), down(high2)
    coded0 = pair_products(place, [(0, 1), (0, 2), (1, 2)], blocks, mine, together=True)
    got0 = [across(coded0[0])]
    low, high, got0 = lax.optimization_barrier((low, high, got0))
    low_a, low_b, other = pieces_for_sibling(place, low, high)
    low_as, low_bs, high_sib = swap((low_a, low_b, other))
    blocks["L"] = [("low", 0)], [("low_as", 0), ("low_bs", 0)]
    blocks["H"] = [("high", 0)], [("high_sib", 0)]
    coded1 = pair_products(
        place,
        [("L", 0), ("L", 1), ("L", 2), (0, "H"), (1, "H"), ("L", "H")],
        blocks,
        mine | {"low": low, "low_as": low_as, "low_bs": low_bs, "high": high, "high_sib": high_sib},
    )
    got1 = to_chips(coded1)
    outs = add_parts(
        place,
        got0,
        [mask],
        None,
        [
            ((0, 0, 0), [("f", 0, 0), ("b", 1, 0)]),
            ((0, 0, 1), [("f", 0, 1), ("b", 2, 1)]),
            ((0, 1, 0), [("f", 1, 0), ("b", 2, 0)]),
        ],
    )
    low2, high2, _, outs = lax.optimization_barrier((low2, high2, coded1[0], outs))
    blocks["H2"] = [("high2", 0)], [("high2", 1)]
    blocks["L2"] = [("low2", 0)], [("low2", 1)]
    *coded2, lines = pair_products(
        place,
        [(0, "H2"), (1, "H2"), ("L2", 2)],
        blocks,
        mine | {"high2": high2, "low2": low2},
        halved=("L2",),
        lines="low2",
    )
    got2 = to_chips(coded2)
    *outs, up1, down1 = add_parts(
        place,
        got1,
        [mask, lines],
        outs,
        [
            ((1, 2, 0), [("b", 0, 0), ("m", 1, 0)]),
            ((1, 2, 1), [("b", 1, 1), ("m", 1, 1)]),
            ((1, 2, 2), [("b", 2, 2), ("m", 1, 2)]),
            ((0, 0, 2), [("f", 0, 2), ("m", 0, 0)]),
            ((0, 1, 1), [("f", 1, 1), ("m", 0, 1)]),
            ((1, 2, 3), [("m", 0, 2), ("m", 1, 3)]),
        ],
        (3, 4),
    )
    below1, above1 = up(up1), down(down1)
    *outs, up2, same, cross, kept, other = add_parts(
        place,
        got2,
        [mask, lines],
        outs,
        [
            ((0, 0, 3), [("f", 0, 3), ("m", 0, 0)]),
            ((0, 1, 2), [("f", 1, 2), ("m", 0, 1)]),
            ((1, 1, 3), [("halves",)]),
        ],
        (2,),
        halves=True,
    )
    below2, same, cross = up(up2), down(same), down_across(cross)
    other = swap(other)
    outs = place_results(
        place,
        [below1, above1],
        [kept, other],
        outs,
        [
            [("b", 0, 2), ("b", 0, 1), ("b", 0, 3)],
            [("f", 2, 0), ("f", 2, 1), ("f", 2, 2), ("f", 2, 3)],
        ],
        [("b", 2, 3)],
    )
    forward, backward = place_results(
        place, [below2], [same, cross], outs, [[("b", 1, 3), ("b", 1, 2)]], [("f", 1, 3)]
    )
    return jnp.swapaxes(forward, 2, 3), backward


def solution(mesh):
    in_specs = (P("space", None, "occ"), P("space", None))
    out_specs = (P("space", None, None, "occ"), P("space", None, "occ", None))
    return jax.shard_map(
        on_device, mesh=mesh, in_specs=in_specs, out_specs=out_specs, check_vma=False
    )
```

```python
import functools

import jax
import jax.numpy as jnp
from jax import lax
from jax.experimental import pallas as pl
from jax.experimental.pallas import tpu as pltpu
from jax.sharding import PartitionSpec as P

BF = 512
COLS = 1024
HALF = 256
SLICE = 64
CHIPS = 4
STEPS = 256.0
TOP = 32700.0
LN2 = 0.6931471805599453

VMEM = pl.BlockSpec(memory_space=pltpu.VMEM)
SMEM = pl.BlockSpec(memory_space=pltpu.SMEM)
HBM = pl.BlockSpec(memory_space=pltpu.HBM)
PARAMS = pltpu.CompilerParams(vmem_limit_bytes=18 << 20)
FAR = pltpu.CompilerParams(vmem_limit_bytes=62 << 20)
OUTS = [jax.ShapeDtypeStruct((3, 4, SLICE, BF), jnp.float32)] * 2


def coded_rows(count):
    return count * SLICE + 16


def code(values):
    tops = jnp.concatenate([jnp.max(jnp.abs(v), 0, keepdims=True) for v in values], 0)
    level = jnp.ceil(jnp.log(jnp.maximum(tops, 1e-30) / TOP) * (STEPS / LN2))
    gain = jnp.exp(level * (-LN2 / STEPS))
    coded = [
        jnp.round(v * gain[i : i + 1]).astype(jnp.int32).astype(jnp.int16)
        for i, v in enumerate(values)
    ]
    return coded, level.astype(jnp.int32)


def level_rows(levels):
    rows = list(levels) + [jnp.zeros((16 - len(levels), BF), jnp.int32)]
    return jnp.concatenate(rows, 0).astype(jnp.int16)


def scales_of(rows):
    return jnp.exp(rows.astype(jnp.float32) * (LN2 / STEPS))


def pair_kernel(pairs, blocks, halved, names, together, late, with_second, place_ref, *refs):
    ins = dict(zip(names, refs))
    outs = refs[len(names) :]
    if with_second:
        outs, mask_ref, second = outs[1:-2], outs[0], outs[-2:]
        put_second(place_ref, mask_ref, (ins["own"], ins["sib"]), *second)
    if late:
        *outs, lines_ref = outs
        first_ref, second_ref = ins["first"], ins["second"]

        def work(low_ref, high_ref):
            ins.update({"low2": low_ref, "high2": high_ref})
            lines_ref[...] = low_ref[0, HALF : HALF + 16, :BF].astype(jnp.float32)
            pair_work(pairs, blocks, halved, ins, outs, together, place_ref)

        @pl.when(place_ref[2] == 1)
        def _():
            work(second_ref, first_ref)

        @pl.when(place_ref[2] == 0)
        def _():
            work(first_ref, second_ref)

        return
    pair_work(pairs, blocks, halved, ins, outs, together, place_ref)


def pair_work(pairs, blocks, halved, ins, outs, together, place_ref):
    if together:
        outs = [outs[0].at[d] for d in range(CHIPS)]
    core, chip = place_ref[0], place_ref[1]
    order = [d if together else (chip + d) % CHIPS for d in range(CHIPS)]

    def read(piece, start, rows):
        name, index = piece
        return ins[name][index, pl.ds(start, rows), :]

    def slices(pieces):
        rows = []
        for o in order:
            if len(pieces) == 2:
                start = (2 * (o % 2) + core) * SLICE
                low, high = (read(piece, start, SLICE) for piece in pieces)
                rows.append(jnp.where(o < 2, low, high))
            elif ins[pieces[0][0]].shape[1] < BF:
                rows.append(read(pieces[0], o * SLICE, SLICE))
            else:
                rows.append(read(pieces[0], (2 * o + core) * SLICE, SLICE))
        return jnp.concatenate(rows, 0)

    def both_slices(pieces):
        rows = [read(pieces[0], o * 2 * SLICE, 2 * SLICE) for o in order]
        return jnp.concatenate(rows, 0)

    def term(a, b, part):
        shared = a in halved
        right = (both_slices if shared else slices)(blocks[b][part])
        pieces = blocks[a][part]
        rows = (HALF if shared else BF) // len(pieces)
        values = [
            lax.dot_general(
                right,
                read(piece, 0, rows),
                (((1,), (1,)), ((), ())),
                preferred_element_type=jnp.float32,
            )
            for piece in pieces
        ]
        return jnp.concatenate(values, 1)

    levels = []
    for p, (a, b) in enumerate(pairs):
        shared = a in halved
        acc = term(a, b, 0) + term(a, b, 1)
        if shared:
            parts = [
                jnp.concatenate(
                    [acc[k * SLICE : (k + 1) * SLICE] for k in (2 * d, 2 * d + 1)], 1
                )
                for d in range(CHIPS)
            ]
        else:
            parts = [acc[d * SLICE : (d + 1) * SLICE] for d in range(CHIPS)]
        coded, level = code(parts)
        for d in range(CHIPS):
            outs[d][p * SLICE : (p + 1) * SLICE, :] = coded[d]
        levels.append(level)
    end = len(pairs) * SLICE
    for d in range(CHIPS):
        outs[d][end : end + 16, :] = level_rows([v[d : d + 1] for v in levels])


def put_second(place_ref, mask_ref, sources, first_ref, second_ref):
    core = place_ref[0]
    lines = [
        jnp.full((1, COLS), mask_ref[k // 4, k % 4].astype(jnp.float32), jnp.float32)
        for k in range(12)
    ]
    lines.append(jnp.zeros((4, COLS), jnp.float32))
    lines = jnp.concatenate(lines, 0).astype(jnp.bfloat16)

    def put(up_ref, down_ref):
        for i, source in enumerate(sources):
            up_ref[i, :HALF, :] = source[1, pl.ds(core * HALF, HALF), :]
            up_ref[i, HALF:, :] = lines
            for y in range(CHIPS):
                down_ref[i, y * SLICE : (y + 1) * SLICE, :] = source[
                    1, pl.ds((2 * y + core) * SLICE, SLICE), :
                ]
            down_ref[i, HALF:, :] = lines

    @pl.when(place_ref[2] == 1)
    def _():
        put(first_ref, second_ref)

    @pl.when(place_ref[2] == 0)
    def _():
        put(second_ref, first_ref)


def pair_products(place, pairs, blocks, operands, halved=(), together=False, late=False, mask=None):
    names = list(operands)
    n = len(pairs)
    rows = coded_rows(n)
    shapes = [jax.ShapeDtypeStruct((rows, BF), jnp.int16)] * CHIPS
    if together:
        shapes = [jax.ShapeDtypeStruct((CHIPS, rows, BF), jnp.int16)]
    if late:
        shapes.append(jax.ShapeDtypeStruct((16, BF), jnp.float32))
    second = mask is not None
    if second:
        shapes += [jax.ShapeDtypeStruct((2, HALF + 16, COLS), jnp.bfloat16)] * 2
    return pl.pallas_call(
        functools.partial(pair_kernel, pairs, blocks, halved, names, together, late, second),
        out_shape=shapes,
        in_specs=[SMEM] + [VMEM] * len(names) + [SMEM] * second,
        out_specs=[VMEM] * len(shapes),
        compiler_params=FAR if together else PARAMS,
        cost_estimate=pl.CostEstimate(flops=1 << 20, bytes_accessed=1 << 16, transcendentals=0),
    )(place, *operands.values(), *([mask] if second else []))


def first_kernel(own_ref, first_ref, second_ref, held, sems):
    n = 4
    rows = BF // n
    odd = lax.axis_index("space") % 2
    copies = []
    for k in range(2 * n):
        at = pl.ds((k % n) * rows, rows)
        block, target = ((2 * odd, first_ref), (2 - 2 * odd, second_ref))[k // n]
        copies.append(
            (
                pltpu.make_async_copy(own_ref.at[block, at], held.at[k], sems.at[0, k]),
                pltpu.make_async_copy(held.at[k], target.at[0, at], sems.at[1, k]),
            )
        )
    for load, _ in copies:
        load.start()
    for load, store in copies:
        load.wait()
        store.start()
    for _, store in copies:
        store.wait()


def first_factors(own):
    return pl.pallas_call(
        first_kernel,
        out_shape=[jax.ShapeDtypeStruct((1, BF, COLS), jnp.bfloat16)] * 2,
        in_specs=[HBM],
        out_specs=[HBM] * 2,
        scratch_shapes=[
            pltpu.VMEM((8, BF // 4, COLS), jnp.bfloat16),
            pltpu.SemaphoreType.DMA((2, 8)),
        ],
        compiler_params=FAR,
        cost_estimate=pl.CostEstimate(flops=1 << 10, bytes_accessed=1 << 10, transcendentals=0),
    )(own)


def bring_kernel(ref, out_ref, sem):
    copy = pltpu.make_async_copy(ref, out_ref, sem)
    copy.start()
    copy.wait()


def bring(value):
    return pl.pallas_call(
        bring_kernel,
        out_shape=jax.ShapeDtypeStruct(value.shape, value.dtype),
        in_specs=[HBM],
        out_specs=VMEM,
        scratch_shapes=[pltpu.SemaphoreType.DMA],
        compiler_params=PARAMS,
        cost_estimate=pl.CostEstimate(flops=1 << 10, bytes_accessed=1 << 10, transcendentals=0),
    )(value)


def arrived_kernel(place_ref, first_ref, second_ref, low_a_ref, low_b_ref, mine_ref, other_ref):
    def put(low_ref, high_ref):
        low_a_ref[0] = low_ref[0, :HALF, :]
        low_b_ref[0] = low_ref[0, HALF:, :]
        for core, target in ((place_ref[0], mine_ref), (1 - place_ref[0], other_ref)):
            for y in range(CHIPS):
                start = (2 * y + core) * SLICE
                target[0, y * SLICE : (y + 1) * SLICE, :] = high_ref[0, pl.ds(start, SLICE), :]

    @pl.when(place_ref[2] == 1)
    def _():
        put(second_ref, first_ref)

    @pl.when(place_ref[2] == 0)
    def _():
        put(first_ref, second_ref)


def arrived(place, first, second):
    return pl.pallas_call(
        arrived_kernel,
        out_shape=[jax.ShapeDtypeStruct((1, HALF, COLS), jnp.bfloat16)] * 4,
        in_specs=[SMEM, VMEM, VMEM],
        out_specs=[VMEM] * 4,
        compiler_params=PARAMS,
        cost_estimate=pl.CostEstimate(flops=1 << 10, bytes_accessed=1 << 10, transcendentals=0),
    )(place, first, second)


def put_messages(place_ref, refs, held):
    def put(refs):
        for ref, blocks in zip(refs, held):
            for k, (coded, _) in enumerate(blocks):
                ref[k * SLICE : (k + 1) * SLICE, :] = coded
            end = ref.shape[0] - 16
            ref[end : end + 16, :] = level_rows([level for _, level in blocks])

    if len(refs) < 2:
        put(refs)
        return

    @pl.when(place_ref[2] == 1)
    def _():
        put(refs)

    @pl.when(place_ref[2] == 0)
    def _():
        put(refs[::-1])


def add_kernel(places, first, sizes, halves, n_gots, lined, place_ref, *refs):
    gots, refs = refs[:n_gots], refs[n_gots:]
    if n_gots == 1:
        gots = [gots[0].at[d] for d in range(CHIPS)]
    mask_ref, refs = refs[0], refs[1:]
    if lined:
        lines_ref, refs = refs[0], refs[1:]
    if not first:
        refs = refs[2:]
    (f_ref, b_ref), refs = refs[:2], refs[2:]
    messages, refs = refs[: len(sizes)], refs[len(sizes) :]
    if halves:
        (kept_ref, swap_ref), refs = refs[:2], refs[2:]
    sums, sems = refs
    held = [[] for _ in sizes]
    writes = []
    n = len(places)
    scales = [scales_of(gots[d][n * SLICE : n * SLICE + 16, :]) for d in range(CHIPS)]
    for p, ((theirs, block, slot), goals) in enumerate(places):
        total = None
        for d in range(CHIPS):
            part = gots[d][p * SLICE : (p + 1) * SLICE, :].astype(jnp.float32)
            part = part * scales[d][p : p + 1]
            total = part if total is None else total + part
        if theirs:
            line = lines_ref[block * 4 + slot : block * 4 + slot + 1, :]
            total = total * line
        else:
            total = total * mask_ref[block, slot].astype(jnp.float32)
        coded = None
        for kind, *goal in goals:
            if kind == "m":
                which, index = goal
                if coded is None:
                    (coded,), level = code([total])
                assert index == len(held[which])
                held[which].append((coded, level))
            elif kind == "halves":
                first_core = place_ref[0] == 0
                low, high = total[:, :HALF], total[:, HALF:]
                kept_ref[...] = jnp.where(first_core, low, high)
                swap_ref[...] = jnp.where(first_core, high, low)
            else:
                sums[p] = total
                writes.append((p, (f_ref if kind == "f" else b_ref).at[goal[0], goal[1]]))
    put_messages(place_ref, messages, held)
    writes = [
        pltpu.make_async_copy(sums.at[p], target, sems.at[k])
        for k, (p, target) in enumerate(writes)
    ]
    for copy in writes:
        copy.start()
    for copy in writes:
        copy.wait()


def add_parts(place, gots, masks, outs, places, sizes=(), halves=False):
    n = len(places)
    first = outs is None
    earlier = [] if first else list(outs)
    at = 1 + len(gots) + len(masks)
    shapes = OUTS + [jax.ShapeDtypeStruct((coded_rows(max(sizes, default=0)), BF), jnp.int16) for _ in sizes]
    if halves:
        shapes += [jax.ShapeDtypeStruct((SLICE, HALF), jnp.float32)] * 2
    return pl.pallas_call(
        functools.partial(add_kernel, places, first, sizes, halves, len(gots), len(masks) > 1),
        out_shape=shapes,
        in_specs=[SMEM] + [VMEM] * len(gots) + [SMEM, VMEM][: len(masks)] + [HBM] * len(earlier),
        out_specs=[HBM] * 2 + [VMEM] * (len(shapes) - 2),
        scratch_shapes=[
            pltpu.VMEM((n, SLICE, BF), jnp.float32),
            pltpu.SemaphoreType.DMA((2 * n,)),
        ],
        input_output_aliases={} if first else {at: 0, at + 1: 1},
        compiler_params=PARAMS,
        cost_estimate=pl.CostEstimate(flops=1 << 20, bytes_accessed=1 << 16, transcendentals=0),
    )(place, *gots, *masks, *earlier)


def place_kernel(below_places, above_places, block_places, place_ref, first_ref, second_ref, *refs):
    blocks, refs = refs[: len(block_places)], refs[len(block_places) + 2 :]
    f_ref, b_ref, sums, sems = refs
    goals = below_places + above_places + block_places

    def take(*messages):
        k = 0
        for ref, count in zip(messages, (len(below_places), len(above_places))):
            end = ref.shape[0] - 16
            scales = scales_of(ref[end : end + 16, :])
            for p in range(count):
                part = ref[p * SLICE : (p + 1) * SLICE, :].astype(jnp.float32)
                sums[k] = part * scales[p : p + 1]
                k += 1

    @pl.when(place_ref[2] == 1)
    def _():
        take(second_ref, first_ref)

    @pl.when(place_ref[2] == 0)
    def _():
        take(first_ref, second_ref)

    for k, block in enumerate(blocks):
        sums[len(goals) - len(blocks) + k] = block[...]
    writes = []
    for k, (kind, block, slot) in enumerate(goals):
        target = (f_ref if kind == "f" else b_ref).at[block, slot]
        writes.append(pltpu.make_async_copy(sums.at[k], target, sems.at[k]))
    for copy in writes:
        copy.start()
    for copy in writes:
        copy.wait()


def place_results(place, first, second, outs, below_places, above_places, blocks=(), block_places=()):
    total = len(below_places) + len(above_places) + len(blocks)
    n = 3 + len(blocks)
    return pl.pallas_call(
        functools.partial(place_kernel, below_places, above_places, list(block_places)),
        out_shape=OUTS,
        in_specs=[SMEM] + [VMEM] * (n - 1) + [HBM] * 2,
        out_specs=[HBM] * 2,
        scratch_shapes=[
            pltpu.VMEM((total, SLICE, BF), jnp.float32),
            pltpu.SemaphoreType.DMA((total,)),
        ],
        input_output_aliases={n: 0, n + 1: 1},
        compiler_params=PARAMS,
        cost_estimate=pl.CostEstimate(flops=1 << 20, bytes_accessed=1 << 16, transcendentals=0),
    )(place, first, second, *blocks, *outs)


def join_kernel(place_ref, mine_ref, other_ref, up_ref, block_ref, *refs):
    first_core = place_ref[0] == 0
    mine, other = mine_ref[...], other_ref[...]
    low, high = jnp.where(first_core, mine, other), jnp.where(first_core, other, mine)
    total = jnp.concatenate([low, high], 1)
    block_ref[...] = total
    (coded,), level = code([total])

    def put(up_to, down_to):
        up_to[...] = up_ref[...]
        end = down_to.shape[0] - 16
        down_to[:SLICE, :] = coded
        down_to[end:, :] = level_rows([level])

    @pl.when(place_ref[2] == 1)
    def _():
        put(*refs)

    @pl.when(place_ref[2] == 0)
    def _():
        put(*refs[::-1])


def join_halves(place, mine, other, up):
    return pl.pallas_call(
        join_kernel,
        out_shape=[
            jax.ShapeDtypeStruct((SLICE, BF), jnp.float32),
            jax.ShapeDtypeStruct(up.shape, jnp.int16),
            jax.ShapeDtypeStruct(up.shape, jnp.int16),
        ],
        in_specs=[SMEM, VMEM, VMEM, VMEM],
        out_specs=[VMEM] * 3,
        compiler_params=PARAMS,
        cost_estimate=pl.CostEstimate(flops=1 << 10, bytes_accessed=1 << 10, transcendentals=0),
    )(place, mine, other, up)


def swap(value):
    return lax.ppermute(value, "occ", [(o, o ^ 1) for o in range(2 * CHIPS)])


def chips_on(value, by):
    pairs = [
        (2 * y + core, 2 * ((y + by) % CHIPS) + core) for y in range(CHIPS) for core in range(2)
    ]
    return lax.ppermute(value, "occ", pairs)


def across(value):
    groups = [[2 * y + core for y in range(CHIPS)] for core in range(2)]
    return lax.all_to_all(value, "occ", 0, 0, axis_index_groups=groups)


def to_chips(parts):
    return [parts[0]] + [chips_on(parts[d], d) for d in range(1, CHIPS)]


def pairwise(first, second):
    size = lax.axis_size("space")
    done = []
    for value, start in ((first, 1), (second, 0)):
        pairs = [(i, i + 1) for i in range(start, size - 1, 2)]
        pairs += [(j, i) for i, j in pairs]
        done.append(lax.ppermute(value, "space", sorted(pairs)))
    return done


def on_device(own, mask):
    index = lax.axis_index("occ")
    place = jnp.stack([index % 2, index // 2, lax.axis_index("space") % 2]).astype(jnp.int32)
    own_sib = swap(own)
    first, second = pairwise(*first_factors(own))
    mine = {"own": own, "sib": own_sib}
    blocks = {k: ([("own", k)], [("sib", k)]) for k in range(3)}
    coded0, first2, second2 = pair_products(
        place, [(0, 1), (0, 2), (1, 2)], blocks, mine, together=True, mask=mask
    )
    first2, second2 = pairwise(first2, second2)
    got0 = [across(coded0)]
    first, second, got0 = lax.optimization_barrier((first, second, got0))
    low_a, low_b, high, other = arrived(place, first, second)
    low_as, low_bs, high_sib = swap((low_a, low_b, other))
    blocks["L"] = [("low_a", 0), ("low_b", 0)], [("low_as", 0), ("low_bs", 0)]
    blocks["H"] = [("high", 0)], [("high_sib", 0)]
    coded1 = pair_products(
        place,
        [("L", 0), ("L", 1), ("L", 2), (0, "H"), (1, "H"), ("L", "H")],
        blocks,
        mine
        | {"low_a": low_a, "low_b": low_b, "low_as": low_as, "low_bs": low_bs}
        | {"high": high, "high_sib": high_sib},
    )
    got1 = to_chips(coded1)
    outs = add_parts(
        place,
        got0,
        [mask],
        None,
        [
            ((0, 0, 0), [("f", 0, 0), ("b", 1, 0)]),
            ((0, 0, 1), [("f", 0, 1), ("b", 2, 1)]),
            ((0, 1, 0), [("f", 1, 0), ("b", 2, 0)]),
        ],
    )
    near, _ = lax.optimization_barrier((own_sib, coded1[0]))
    near = bring(near)
    first2, second2, _, outs, near = lax.optimization_barrier((first2, second2, coded1[0], outs, near))
    blocks["H2"] = [("high2", 0)], [("high2", 1)]
    blocks["L2"] = [("low2", 0)], [("low2", 1)]
    *coded2, lines = pair_products(
        place,
        [(0, "H2"), (1, "H2"), ("L2", 2)],
        blocks,
        {"own": own, "sib": near} | {"first": first2, "second": second2},
        halved=("L2",),
        late=True,
    )
    got2 = to_chips(coded2)
    *outs, up1, down1 = add_parts(
        place,
        got1,
        [mask, lines],
        outs,
        [
            ((1, 2, 0), [("b", 0, 0), ("m", 1, 0)]),
            ((1, 2, 1), [("b", 1, 1), ("m", 1, 1)]),
            ((1, 2, 2), [("b", 2, 2), ("m", 1, 2)]),
            ((0, 0, 2), [("f", 0, 2), ("m", 0, 0)]),
            ((0, 1, 1), [("f", 1, 1), ("m", 0, 1)]),
            ((1, 2, 3), [("m", 0, 2), ("m", 1, 3)]),
        ],
        (3, 4),
    )
    first3, second3 = pairwise(up1, down1)
    *outs, up2, mine_half, other_half = add_parts(
        place,
        got2,
        [mask, lines],
        outs,
        [
            ((0, 0, 3), [("f", 0, 3), ("m", 0, 0)]),
            ((0, 1, 2), [("f", 1, 2), ("m", 0, 1)]),
            ((1, 1, 3), [("halves",)]),
        ],
        (2,),
        halves=True,
    )
    block, first4, second4 = join_halves(place, mine_half, swap(other_half), up2)
    first4, second4 = pairwise(first4, second4)
    outs = place_results(
        place,
        first3,
        second3,
        outs,
        [("b", 0, 2), ("b", 0, 1), ("b", 0, 3)],
        [("f", 2, 0), ("f", 2, 1), ("f", 2, 2), ("f", 2, 3)],
        [block],
        [("b", 2, 3)],
    )
    forward, backward = place_results(
        place, first4, second4, outs, [("b", 1, 3), ("b", 1, 2)], [("f", 1, 3)]
    )
    return jnp.swapaxes(forward, 2, 3), backward


def solution(mesh):
    in_specs = (P("space", None, "occ"), P("space", None))
    out_specs = (P("space", None, None, "occ"), P("space", None, "occ", None))
    return jax.shard_map(
        on_device, mesh=mesh, in_specs=in_specs, out_specs=out_specs, check_vma=False
    )
```

```python
import functools

import jax
import jax.numpy as jnp
from jax import lax
from jax.experimental import pallas as pl
from jax.experimental.pallas import tpu as pltpu
from jax.sharding import PartitionSpec as P

BF = 512
COLS = 1024
HALF = 256
SLICE = 64
CHIPS = 4
STEPS = 256.0
TOP = 32700.0
LN2 = 0.6931471805599453

VMEM = pl.BlockSpec(memory_space=pltpu.VMEM)
SMEM = pl.BlockSpec(memory_space=pltpu.SMEM)
HBM = pl.BlockSpec(memory_space=pltpu.HBM)
PARAMS = pltpu.CompilerParams(vmem_limit_bytes=18 << 20)
FAR = pltpu.CompilerParams(vmem_limit_bytes=62 << 20)
OUTS = [jax.ShapeDtypeStruct((3, 4, SLICE, BF), jnp.float32)] * 2


def coded_rows(count):
    return count * SLICE + 16


def code(values):
    tops = jnp.concatenate([jnp.max(jnp.abs(v), 0, keepdims=True) for v in values], 0)
    level = jnp.ceil(jnp.log(jnp.maximum(tops, 1e-30) / TOP) * (STEPS / LN2))
    gain = jnp.exp(level * (-LN2 / STEPS))
    coded = [
        jnp.round(v * gain[i : i + 1]).astype(jnp.int32).astype(jnp.int16)
        for i, v in enumerate(values)
    ]
    return coded, level.astype(jnp.int32)


def level_rows(levels):
    rows = list(levels) + [jnp.zeros((16 - len(levels), BF), jnp.int32)]
    return jnp.concatenate(rows, 0).astype(jnp.int16)


def scales_of(rows):
    return jnp.exp(rows.astype(jnp.float32) * (LN2 / STEPS))


def pair_kernel(pairs, blocks, halved, names, together, late, with_second, place_ref, *refs):
    ins = dict(zip(names, refs))
    outs = refs[len(names) :]
    if with_second:
        outs, mask_ref, second = outs[1:-2], outs[0], outs[-2:]
        put_second(place_ref, mask_ref, (ins["own"], ins["sib"]), *second)
    if late:
        *outs, lines_ref = outs
        first_ref, second_ref = ins["first"], ins["second"]

        def work(low_ref, high_ref):
            ins.update({"low2": low_ref, "high2": high_ref})
            lines_ref[...] = low_ref[0, HALF : HALF + 16, :BF].astype(jnp.float32)
            pair_work(pairs, blocks, halved, ins, outs, together, place_ref)

        @pl.when(place_ref[2] == 1)
        def _():
            work(second_ref, first_ref)

        @pl.when(place_ref[2] == 0)
        def _():
            work(first_ref, second_ref)

        return
    pair_work(pairs, blocks, halved, ins, outs, together, place_ref)


def pair_work(pairs, blocks, halved, ins, outs, together, place_ref):
    if together:
        outs = [outs[0].at[d] for d in range(CHIPS)]
    core, chip = place_ref[0], place_ref[1]
    order = [d if together else (chip + d) % CHIPS for d in range(CHIPS)]

    def read(piece, start, rows):
        name, index = piece
        return ins[name][index, pl.ds(start, rows), :]

    def slices(pieces):
        rows = []
        for o in order:
            if len(pieces) == 2:
                start = (2 * (o % 2) + core) * SLICE
                low, high = (read(piece, start, SLICE) for piece in pieces)
                rows.append(jnp.where(o < 2, low, high))
            elif ins[pieces[0][0]].shape[1] < BF:
                rows.append(read(pieces[0], o * SLICE, SLICE))
            else:
                rows.append(read(pieces[0], (2 * o + core) * SLICE, SLICE))
        return jnp.concatenate(rows, 0)

    def both_slices(pieces):
        rows = [read(pieces[0], o * 2 * SLICE, 2 * SLICE) for o in order]
        return jnp.concatenate(rows, 0)

    def term(a, b, part):
        shared = a in halved
        right = (both_slices if shared else slices)(blocks[b][part])
        pieces = blocks[a][part]
        rows = (HALF if shared else BF) // len(pieces)
        values = [
            lax.dot_general(
                right,
                read(piece, 0, rows),
                (((1,), (1,)), ((), ())),
                preferred_element_type=jnp.float32,
            )
            for piece in pieces
        ]
        return jnp.concatenate(values, 1)

    levels = []
    for p, (a, b) in enumerate(pairs):
        shared = a in halved
        acc = term(a, b, 0) + term(a, b, 1)
        if shared:
            parts = [
                jnp.concatenate(
                    [acc[k * SLICE : (k + 1) * SLICE] for k in (2 * d, 2 * d + 1)], 1
                )
                for d in range(CHIPS)
            ]
        else:
            parts = [acc[d * SLICE : (d + 1) * SLICE] for d in range(CHIPS)]
        coded, level = code(parts)
        for d in range(CHIPS):
            outs[d][p * SLICE : (p + 1) * SLICE, :] = coded[d]
        levels.append(level)
    end = len(pairs) * SLICE
    for d in range(CHIPS):
        outs[d][end : end + 16, :] = level_rows([v[d : d + 1] for v in levels])


def put_second(place_ref, mask_ref, sources, first_ref, second_ref):
    core = place_ref[0]
    lines = [
        jnp.full((1, COLS), mask_ref[k // 4, k % 4].astype(jnp.float32), jnp.float32)
        for k in range(12)
    ]
    lines.append(jnp.zeros((4, COLS), jnp.float32))
    lines = jnp.concatenate(lines, 0).astype(jnp.bfloat16)

    def put(up_ref, down_ref):
        for i, source in enumerate(sources):
            up_ref[i, :HALF, :] = source[1, pl.ds(core * HALF, HALF), :]
            up_ref[i, HALF:, :] = lines
            for y in range(CHIPS):
                down_ref[i, y * SLICE : (y + 1) * SLICE, :] = source[
                    1, pl.ds((2 * y + core) * SLICE, SLICE), :
                ]
            down_ref[i, HALF:, :] = lines

    @pl.when(place_ref[2] == 1)
    def _():
        put(first_ref, second_ref)

    @pl.when(place_ref[2] == 0)
    def _():
        put(second_ref, first_ref)


def pair_products(place, pairs, blocks, operands, halved=(), together=False, late=False, mask=None):
    names = list(operands)
    n = len(pairs)
    rows = coded_rows(n)
    shapes = [jax.ShapeDtypeStruct((rows, BF), jnp.int16)] * CHIPS
    if together:
        shapes = [jax.ShapeDtypeStruct((CHIPS, rows, BF), jnp.int16)]
    if late:
        shapes.append(jax.ShapeDtypeStruct((16, BF), jnp.float32))
    second = mask is not None
    if second:
        shapes += [jax.ShapeDtypeStruct((2, HALF + 16, COLS), jnp.bfloat16)] * 2
    return pl.pallas_call(
        functools.partial(pair_kernel, pairs, blocks, halved, names, together, late, second),
        out_shape=shapes,
        in_specs=[SMEM] + [VMEM] * len(names) + [SMEM] * second,
        out_specs=[VMEM] * len(shapes),
        compiler_params=FAR if together else PARAMS,
        cost_estimate=pl.CostEstimate(flops=1 << 20, bytes_accessed=1 << 16, transcendentals=0),
    )(place, *operands.values(), *([mask] if second else []))


def first_kernel(own_ref, first_ref, second_ref, held, sems):
    n = 4
    rows = BF // n
    odd = lax.axis_index("space") % 2
    copies = []
    for k in range(2 * n):
        at = pl.ds((k % n) * rows, rows)
        block, target = ((2 * odd, first_ref), (2 - 2 * odd, second_ref))[k // n]
        copies.append(
            (
                pltpu.make_async_copy(own_ref.at[block, at], held.at[k], sems.at[0, k]),
                pltpu.make_async_copy(held.at[k], target.at[0, at], sems.at[1, k]),
            )
        )
    for load, _ in copies:
        load.start()
    for load, store in copies:
        load.wait()
        store.start()
    for _, store in copies:
        store.wait()


def first_factors(own):
    return pl.pallas_call(
        first_kernel,
        out_shape=[jax.ShapeDtypeStruct((1, BF, COLS), jnp.bfloat16)] * 2,
        in_specs=[HBM],
        out_specs=[HBM] * 2,
        scratch_shapes=[
            pltpu.VMEM((8, BF // 4, COLS), jnp.bfloat16),
            pltpu.SemaphoreType.DMA((2, 8)),
        ],
        compiler_params=FAR,
        cost_estimate=pl.CostEstimate(flops=1 << 10, bytes_accessed=1 << 10, transcendentals=0),
    )(own)


def bring_kernel(ref, out_ref, sem):
    copy = pltpu.make_async_copy(ref, out_ref, sem)
    copy.start()
    copy.wait()


def bring(value):
    return pl.pallas_call(
        bring_kernel,
        out_shape=jax.ShapeDtypeStruct(value.shape, value.dtype),
        in_specs=[HBM],
        out_specs=VMEM,
        scratch_shapes=[pltpu.SemaphoreType.DMA],
        compiler_params=PARAMS,
        cost_estimate=pl.CostEstimate(flops=1 << 10, bytes_accessed=1 << 10, transcendentals=0),
    )(value)


def arrived_kernel(place_ref, first_ref, second_ref, low_a_ref, low_b_ref, mine_ref, other_ref):
    def put(low_ref, high_ref):
        low_a_ref[0] = low_ref[0, :HALF, :]
        low_b_ref[0] = low_ref[0, HALF:, :]
        for core, target in ((place_ref[0], mine_ref), (1 - place_ref[0], other_ref)):
            for y in range(CHIPS):
                start = (2 * y + core) * SLICE
                target[0, y * SLICE : (y + 1) * SLICE, :] = high_ref[0, pl.ds(start, SLICE), :]

    @pl.when(place_ref[2] == 1)
    def _():
        put(second_ref, first_ref)

    @pl.when(place_ref[2] == 0)
    def _():
        put(first_ref, second_ref)


def arrived(place, first, second):
    return pl.pallas_call(
        arrived_kernel,
        out_shape=[jax.ShapeDtypeStruct((1, HALF, COLS), jnp.bfloat16)] * 4,
        in_specs=[SMEM, VMEM, VMEM],
        out_specs=[VMEM] * 4,
        compiler_params=PARAMS,
        cost_estimate=pl.CostEstimate(flops=1 << 10, bytes_accessed=1 << 10, transcendentals=0),
    )(place, first, second)


def put_messages(place_ref, refs, held):
    def put(refs):
        for ref, blocks in zip(refs, held):
            for k, (coded, _) in enumerate(blocks):
                ref[k * SLICE : (k + 1) * SLICE, :] = coded
            end = ref.shape[0] - 16
            ref[end : end + 16, :] = level_rows([level for _, level in blocks])

    if len(refs) < 2:
        put(refs)
        return

    @pl.when(place_ref[2] == 1)
    def _():
        put(refs)

    @pl.when(place_ref[2] == 0)
    def _():
        put(refs[::-1])


def add_kernel(places, first, sizes, halves, n_gots, lined, place_ref, *refs):
    gots, refs = refs[:n_gots], refs[n_gots:]
    if n_gots == 1:
        gots = [gots[0].at[d] for d in range(CHIPS)]
    mask_ref, refs = refs[0], refs[1:]
    if lined:
        lines_ref, refs = refs[0], refs[1:]
    if halves:
        messages, (sums, kept_ref, swap_ref) = refs[: len(sizes)], refs[len(sizes) :]
    else:
        if not first:
            refs = refs[2:]
        (f_ref, b_ref), refs = refs[:2], refs[2:]
        messages, (sums, sems) = refs[: len(sizes)], refs[len(sizes) :]
    held = [[] for _ in sizes]
    writes = []
    n = len(places)
    scales = [scales_of(gots[d][n * SLICE : n * SLICE + 16, :]) for d in range(CHIPS)]
    for p, ((theirs, block, slot), goals) in enumerate(places):
        total = None
        for d in range(CHIPS):
            part = gots[d][p * SLICE : (p + 1) * SLICE, :].astype(jnp.float32)
            part = part * scales[d][p : p + 1]
            total = part if total is None else total + part
        if theirs:
            line = lines_ref[block * 4 + slot : block * 4 + slot + 1, :]
            total = total * line
        else:
            total = total * mask_ref[block, slot].astype(jnp.float32)
        coded = None
        for kind, *goal in goals:
            if kind == "m":
                which, index = goal
                if coded is None:
                    (coded,), level = code([total])
                assert index == len(held[which])
                held[which].append((coded, level))
            elif kind == "halves":
                first_core = place_ref[0] == 0
                low, high = total[:, :HALF], total[:, HALF:]
                kept_ref[...] = jnp.where(first_core, low, high)
                swap_ref[...] = jnp.where(first_core, high, low)
            elif kind == "kept":
                sums[goal[0]] = total
            else:
                sums[p] = total
                writes.append((p, (f_ref if kind == "f" else b_ref).at[goal[0], goal[1]]))
    put_messages(place_ref, messages, held)
    writes = [
        pltpu.make_async_copy(sums.at[p], target, sems.at[k])
        for k, (p, target) in enumerate(writes)
    ]
    for copy in writes:
        copy.start()
    for copy in writes:
        copy.wait()


def add_parts(place, gots, masks, outs, places, sizes=(), kept=None):
    n = len(places)
    ins = [place, *gots, *masks]
    messages = [jax.ShapeDtypeStruct((coded_rows(max(sizes, default=0)), BF), jnp.int16)] * len(sizes)
    in_specs = [SMEM] + [VMEM] * len(gots) + [SMEM, VMEM][: len(masks)]
    scratch, aliases = [], {}
    if kept is not None:
        shapes = messages + [jax.ShapeDtypeStruct((kept, SLICE, BF), jnp.float32)]
        shapes += [jax.ShapeDtypeStruct((SLICE, HALF), jnp.float32)] * 2
        out_specs = [VMEM] * len(shapes)
    else:
        shapes = OUTS + messages
        out_specs = [HBM] * 2 + [VMEM] * len(messages)
        scratch = [pltpu.VMEM((n, SLICE, BF), jnp.float32), pltpu.SemaphoreType.DMA((2 * n,))]
        if outs is not None:
            aliases = {len(ins): 0, len(ins) + 1: 1}
            ins += outs
            in_specs += [HBM] * 2
    kernel = functools.partial(
        add_kernel, places, outs is None, sizes, kept is not None, len(gots), len(masks) > 1
    )
    return pl.pallas_call(
        kernel,
        out_shape=shapes,
        in_specs=in_specs,
        out_specs=out_specs,
        scratch_shapes=scratch,
        input_output_aliases=aliases,
        compiler_params=PARAMS,
        cost_estimate=pl.CostEstimate(flops=1 << 20, bytes_accessed=1 << 16, transcendentals=0),
    )(*ins)


def place_kernel(below_places, above_places, block_places, n, place_ref, first_ref, second_ref, *refs):
    blocks, refs = refs[:n], refs[n + 2 :]
    f_ref, b_ref, sums, sems = refs
    odd = place_ref[2] == 1
    end = first_ref.shape[0] - 16
    scales = [scales_of(ref[end : end + 16, :]) for ref in (first_ref, second_ref)]
    writes = []

    def write(source, goal):
        kind, block, slot = goal
        target = (f_ref if kind == "f" else b_ref).at[block, slot]
        writes.append(pltpu.make_async_copy(source, target, sems.at[len(writes)]))
        writes[-1].start()

    goals = iter(block_places)
    for ref in blocks:
        for source in [ref] if len(ref.shape) == 2 else [ref.at[k] for k in range(ref.shape[0])]:
            write(source, next(goals))
    k = 0
    for p in range(max(len(below_places), len(above_places))):
        rows = slice(p * SLICE, (p + 1) * SLICE)
        first, second = (
            ref[rows, :].astype(jnp.float32) * scale[p : p + 1]
            for ref, scale in zip((first_ref, second_ref), scales)
        )
        for places, values in ((below_places, (second, first)), (above_places, (first, second))):
            if p < len(places):
                sums[k] = jnp.where(odd, *values)
                write(sums.at[k], places[p])
                k += 1
    for copy in writes:
        copy.wait()


def place_results(place, first, second, outs, below_places, above_places, blocks=(), block_places=()):
    total = len(below_places) + len(above_places)
    n = 3 + len(blocks)
    return pl.pallas_call(
        functools.partial(place_kernel, below_places, above_places, block_places, len(blocks)),
        out_shape=OUTS,
        in_specs=[SMEM] + [VMEM] * (n - 1) + [HBM] * 2,
        out_specs=[HBM] * 2,
        scratch_shapes=[
            pltpu.VMEM((total, SLICE, BF), jnp.float32),
            pltpu.SemaphoreType.DMA((total + len(block_places),)),
        ],
        input_output_aliases={n: 0, n + 1: 1},
        compiler_params=PARAMS,
        cost_estimate=pl.CostEstimate(flops=1 << 20, bytes_accessed=1 << 16, transcendentals=0),
    )(place, first, second, *blocks, *outs)


def join_kernel(place_ref, mine_ref, other_ref, up_ref, block_ref, *refs):
    first_core = place_ref[0] == 0
    mine, other = mine_ref[...], other_ref[...]
    low, high = jnp.where(first_core, mine, other), jnp.where(first_core, other, mine)
    total = jnp.concatenate([low, high], 1)
    block_ref[...] = total
    (coded,), level = code([total])

    def put(up_to, down_to):
        up_to[...] = up_ref[...]
        end = down_to.shape[0] - 16
        down_to[:SLICE, :] = coded
        down_to[end:, :] = level_rows([level])

    @pl.when(place_ref[2] == 1)
    def _():
        put(*refs)

    @pl.when(place_ref[2] == 0)
    def _():
        put(*refs[::-1])


def join_halves(place, mine, other, up):
    return pl.pallas_call(
        join_kernel,
        out_shape=[
            jax.ShapeDtypeStruct((SLICE, BF), jnp.float32),
            jax.ShapeDtypeStruct(up.shape, jnp.int16),
            jax.ShapeDtypeStruct(up.shape, jnp.int16),
        ],
        in_specs=[SMEM, VMEM, VMEM, VMEM],
        out_specs=[VMEM] * 3,
        compiler_params=PARAMS,
        cost_estimate=pl.CostEstimate(flops=1 << 10, bytes_accessed=1 << 10, transcendentals=0),
    )(place, mine, other, up)


def swap(value):
    return lax.ppermute(value, "occ", [(o, o ^ 1) for o in range(2 * CHIPS)])


def chips_on(value, by):
    pairs = [
        (2 * y + core, 2 * ((y + by) % CHIPS) + core) for y in range(CHIPS) for core in range(2)
    ]
    return lax.ppermute(value, "occ", pairs)


def across(value):
    groups = [[2 * y + core for y in range(CHIPS)] for core in range(2)]
    return lax.all_to_all(value, "occ", 0, 0, axis_index_groups=groups)


def to_chips(parts):
    return [parts[0]] + [chips_on(parts[d], d) for d in range(1, CHIPS)]


def pairwise(first, second):
    size = lax.axis_size("space")
    done = []
    for value, start in ((first, 1), (second, 0)):
        pairs = [(i, i + 1) for i in range(start, size - 1, 2)]
        pairs += [(j, i) for i, j in pairs]
        done.append(lax.ppermute(value, "space", sorted(pairs)))
    return done


def on_device(own, mask):
    index = lax.axis_index("occ")
    place = jnp.stack([index % 2, index // 2, lax.axis_index("space") % 2]).astype(jnp.int32)
    own_sib = swap(own)
    first, second = pairwise(*first_factors(own))
    mine = {"own": own, "sib": own_sib}
    blocks = {k: ([("own", k)], [("sib", k)]) for k in range(3)}
    coded0, first2, second2 = pair_products(
        place, [(0, 1), (0, 2), (1, 2)], blocks, mine, together=True, mask=mask
    )
    first2, second2 = pairwise(first2, second2)
    got0 = [across(coded0)]
    first, second, got0 = lax.optimization_barrier((first, second, got0))
    low_a, low_b, high, other = arrived(place, first, second)
    low_as, low_bs, high_sib = swap((low_a, low_b, other))
    blocks["L"] = [("low_a", 0), ("low_b", 0)], [("low_as", 0), ("low_bs", 0)]
    blocks["H"] = [("high", 0)], [("high_sib", 0)]
    near, _ = lax.optimization_barrier((own_sib, low_a))
    coded1 = pair_products(
        place,
        [("L", 0), ("L", 1), ("L", 2), (0, "H"), (1, "H"), ("L", "H")],
        blocks,
        {"own": own, "sib": bring(near)}
        | {"low_a": low_a, "low_b": low_b, "low_as": low_as, "low_bs": low_bs}
        | {"high": high, "high_sib": high_sib},
    )
    got1 = to_chips(coded1)
    outs = add_parts(
        place,
        got0,
        [mask],
        None,
        [
            ((0, 0, 0), [("f", 0, 0), ("b", 1, 0)]),
            ((0, 0, 1), [("f", 0, 1), ("b", 2, 1)]),
            ((0, 1, 0), [("f", 1, 0), ("b", 2, 0)]),
        ],
    )
    near, _ = lax.optimization_barrier((own_sib, coded1[0]))
    near = bring(near)
    first2, second2, _, outs, near = lax.optimization_barrier((first2, second2, coded1[0], outs, near))
    blocks["H2"] = [("high2", 0)], [("high2", 1)]
    blocks["L2"] = [("low2", 0)], [("low2", 1)]
    *coded2, lines = pair_products(
        place,
        [(0, "H2"), (1, "H2"), ("L2", 2)],
        blocks,
        {"own": own, "sib": near} | {"first": first2, "second": second2},
        halved=("L2",),
        late=True,
    )
    got2 = to_chips(coded2)
    *outs, up1, down1 = add_parts(
        place,
        got1,
        [mask, lines],
        outs,
        [
            ((1, 2, 0), [("b", 0, 0), ("m", 1, 0)]),
            ((1, 2, 1), [("b", 1, 1), ("m", 1, 1)]),
            ((1, 2, 2), [("b", 2, 2), ("m", 1, 2)]),
            ((0, 0, 2), [("f", 0, 2), ("m", 0, 0)]),
            ((0, 1, 1), [("f", 1, 1), ("m", 0, 1)]),
            ((1, 2, 3), [("m", 0, 2), ("m", 1, 3)]),
        ],
        (3, 4),
    )
    first3, second3 = pairwise(up1, down1)
    up2, kept, mine_half, other_half = add_parts(
        place,
        got2,
        [mask, lines],
        None,
        [
            ((0, 0, 3), [("kept", 0), ("m", 0, 0)]),
            ((0, 1, 2), [("kept", 1), ("m", 0, 1)]),
            ((1, 1, 3), [("halves",)]),
        ],
        (2,),
        kept=2,
    )
    block, first4, second4 = join_halves(place, mine_half, swap(other_half), up2)
    first4, second4 = pairwise(first4, second4)
    outs = place_results(
        place,
        first3,
        second3,
        outs,
        [("b", 0, 2), ("b", 0, 1), ("b", 0, 3)],
        [("f", 2, 0), ("f", 2, 1), ("f", 2, 2), ("f", 2, 3)],
        [block, kept],
        [("b", 2, 3), ("f", 0, 3), ("f", 1, 2)],
    )
    forward, backward = place_results(
        place, first4, second4, outs, [("b", 1, 3), ("b", 1, 2)], [("f", 1, 3)]
    )
    return jnp.swapaxes(forward, 2, 3), backward


def solution(mesh):
    in_specs = (P("space", None, "occ"), P("space", None))
    out_specs = (P("space", None, None, "occ"), P("space", None, "occ", None))
    return jax.shard_map(
        on_device, mesh=mesh, in_specs=in_specs, out_specs=out_specs, check_vma=False
    )
```

```python
import functools

import jax
import jax.numpy as jnp
from jax import lax
from jax.experimental import pallas as pl
from jax.experimental.pallas import tpu as pltpu
from jax.sharding import PartitionSpec as P

BF = 512
COLS = 1024
HALF = 256
SLICE = 64
CHIPS = 4
STEPS = 256.0
TOP = 32700.0
LN2 = 0.6931471805599453

VMEM = pl.BlockSpec(memory_space=pltpu.VMEM)
SMEM = pl.BlockSpec(memory_space=pltpu.SMEM)
HBM = pl.BlockSpec(memory_space=pltpu.HBM)
PARAMS = pltpu.CompilerParams(vmem_limit_bytes=18 << 20)
FAR = pltpu.CompilerParams(vmem_limit_bytes=62 << 20)
OUTS = [jax.ShapeDtypeStruct((3, 4, SLICE, BF), jnp.float32)] * 2


def here():
    member = lax.axis_index("occ")
    return member & 1, member >> 1, lax.axis_index("space") & 1


def coded_rows(count):
    return count * SLICE + 16


def code(values):
    tops = jnp.concatenate([jnp.max(jnp.abs(v), 0, keepdims=True) for v in values], 0)
    level = jnp.ceil(jnp.log(jnp.maximum(tops, 1e-30) / TOP) * (STEPS / LN2))
    gain = jnp.exp(level * (-LN2 / STEPS))
    coded = [
        jnp.round(v * gain[i : i + 1]).astype(jnp.int32).astype(jnp.int16)
        for i, v in enumerate(values)
    ]
    return coded, level.astype(jnp.int32)


def level_rows(levels):
    rows = list(levels) + [jnp.zeros((16 - len(levels), BF), jnp.int32)]
    return jnp.concatenate(rows, 0).astype(jnp.int16)


def scales_of(rows):
    return jnp.exp(rows.astype(jnp.float32) * (LN2 / STEPS))


def pair_kernel(pairs, blocks, halved, names, together, late, with_second, *refs):
    place = here()
    ins = dict(zip(names, refs))
    outs = refs[len(names) :]
    if with_second:
        outs, mask_ref, second = outs[1:-2], outs[0], outs[-2:]
        put_second(place, mask_ref, (ins["own"], ins["sib"]), *second)
    if late:
        *outs, lines_ref = outs
        first_ref, second_ref = ins["first"], ins["second"]

        def work(low_ref, high_ref):
            ins.update({"low2": low_ref, "high2": high_ref})
            lines_ref[...] = low_ref[0, HALF : HALF + 16, :BF].astype(jnp.float32)
            pair_work(pairs, blocks, halved, ins, outs, together, place)

        @pl.when(place[2] == 1)
        def _():
            work(second_ref, first_ref)

        @pl.when(place[2] == 0)
        def _():
            work(first_ref, second_ref)

        return
    pair_work(pairs, blocks, halved, ins, outs, together, place)


def pair_work(pairs, blocks, halved, ins, outs, together, place):
    if together:
        outs = [outs[0].at[d] for d in range(CHIPS)]
    core, chip = place[0], place[1]
    order = [d if together else (chip + d) % CHIPS for d in range(CHIPS)]

    def read(piece, start, rows):
        name, index = piece
        return ins[name][index, pl.ds(start, rows), :]

    def slices(pieces):
        rows = []
        for o in order:
            if len(pieces) == 2:
                start = (2 * (o % 2) + core) * SLICE
                low, high = (read(piece, start, SLICE) for piece in pieces)
                rows.append(jnp.where(o < 2, low, high))
            elif ins[pieces[0][0]].shape[1] < BF:
                rows.append(read(pieces[0], o * SLICE, SLICE))
            else:
                rows.append(read(pieces[0], (2 * o + core) * SLICE, SLICE))
        return jnp.concatenate(rows, 0)

    def both_slices(pieces):
        rows = [read(pieces[0], o * 2 * SLICE, 2 * SLICE) for o in order]
        return jnp.concatenate(rows, 0)

    def term(a, b, part):
        shared = a in halved
        right = (both_slices if shared else slices)(blocks[b][part])
        pieces = blocks[a][part]
        rows = (HALF if shared else BF) // len(pieces)
        values = [
            lax.dot_general(
                right,
                read(piece, 0, rows),
                (((1,), (1,)), ((), ())),
                preferred_element_type=jnp.float32,
            )
            for piece in pieces
        ]
        return jnp.concatenate(values, 1)

    levels = []
    for p, (a, b) in enumerate(pairs):
        shared = a in halved
        acc = term(a, b, 0) + term(a, b, 1)
        if shared:
            parts = [
                jnp.concatenate(
                    [acc[k * SLICE : (k + 1) * SLICE] for k in (2 * d, 2 * d + 1)], 1
                )
                for d in range(CHIPS)
            ]
        else:
            parts = [acc[d * SLICE : (d + 1) * SLICE] for d in range(CHIPS)]
        coded, level = code(parts)
        if shared:
            for k in range(2):

                @pl.when(core == k)
                def _():
                    for d in range(CHIPS):
                        row = level_rows([level[d : d + 1]])
                        for ref, j in zip(outs[CHIPS:], (k, 1 - k)):
                            lanes = slice(j * HALF, (j + 1) * HALF)
                            ref[d, :SLICE, :] = coded[d][:, lanes]
                            ref[d, SLICE:, :] = row[:, lanes]

            continue
        for d in range(CHIPS):
            outs[d][p * SLICE : (p + 1) * SLICE, :] = coded[d]
        levels.append(level)
    end = len(levels) * SLICE
    for d in range(CHIPS):
        outs[d][end : end + 16, :] = level_rows([v[d : d + 1] for v in levels])


def put_second(place, mask_ref, sources, first_ref, second_ref):
    core = place[0]
    lines = [
        jnp.full((1, COLS), mask_ref[k // 4, k % 4].astype(jnp.float32), jnp.float32)
        for k in range(12)
    ]
    lines.append(jnp.zeros((4, COLS), jnp.float32))
    lines = jnp.concatenate(lines, 0).astype(jnp.bfloat16)

    def put(up_ref, down_ref):
        for i, source in enumerate(sources):
            up_ref[i, :HALF, :] = source[1, pl.ds(core * HALF, HALF), :]
            up_ref[i, HALF:, :] = lines
            for y in range(CHIPS):
                down_ref[i, y * SLICE : (y + 1) * SLICE, :] = source[
                    1, pl.ds((2 * y + core) * SLICE, SLICE), :
                ]
            down_ref[i, HALF:, :] = lines

    @pl.when(place[2] == 1)
    def _():
        put(first_ref, second_ref)

    @pl.when(place[2] == 0)
    def _():
        put(second_ref, first_ref)


def pair_products(pairs, blocks, operands, halved=(), together=False, late=False, mask=None):
    names = list(operands)
    rows = coded_rows(len(pairs) - len(halved))
    shapes = [jax.ShapeDtypeStruct((rows, BF), jnp.int16)] * CHIPS
    if together:
        shapes = [jax.ShapeDtypeStruct((CHIPS, rows, BF), jnp.int16)]
    if halved:
        shapes += [jax.ShapeDtypeStruct((CHIPS, SLICE + 16, HALF), jnp.int16)] * 2
    if late:
        shapes.append(jax.ShapeDtypeStruct((16, BF), jnp.float32))
    second = mask is not None
    if second:
        shapes += [jax.ShapeDtypeStruct((2, HALF + 16, COLS), jnp.bfloat16)] * 2
    return pl.pallas_call(
        functools.partial(pair_kernel, pairs, blocks, halved, names, together, late, second),
        out_shape=shapes,
        in_specs=[VMEM] * len(names) + [SMEM] * second,
        out_specs=[VMEM] * len(shapes),
        compiler_params=FAR if together else PARAMS,
        cost_estimate=pl.CostEstimate(flops=1 << 20, bytes_accessed=1 << 16, transcendentals=0),
    )(*operands.values(), *([mask] if second else []))


def whole_kernel(*refs):
    place = here()
    coded, (mine_ref, other_ref), outs = refs[:CHIPS], refs[CHIPS : CHIPS + 2], refs[CHIPS + 2 :]
    for d in range(CHIPS):
        end = coded[d].shape[0] - 16
        outs[d][:end, :] = coded[d][:end, :]
        levels = coded[d][end : end + 16, :].astype(jnp.int32)
        for k in range(2):

            @pl.when(place[0] == k)
            def _():
                refs = (mine_ref, other_ref) if k == 0 else (other_ref, mine_ref)
                block = jnp.concatenate([ref[d, :SLICE, :] for ref in refs], 1)
                outs[d][end : end + SLICE, :] = block
                row = [ref[d, SLICE:, :].astype(jnp.int32)[:1] for ref in refs]
                rows = [levels[i : i + 1] for i in range(end // SLICE)]
                rows.append(jnp.concatenate(row, 1))
                outs[d][end + SLICE :, :] = level_rows(rows)


def whole(coded, mine, other):
    rows = coded[0].shape[0] + SLICE
    return pl.pallas_call(
        whole_kernel,
        out_shape=[jax.ShapeDtypeStruct((rows, BF), jnp.int16)] * CHIPS,
        in_specs=[VMEM] * (CHIPS + 2),
        out_specs=[VMEM] * CHIPS,
        compiler_params=PARAMS,
        cost_estimate=pl.CostEstimate(flops=1 << 10, bytes_accessed=1 << 10, transcendentals=0),
    )(*coded, mine, other)


def first_kernel(own_ref, first_ref, second_ref, held, sems):
    n = 4
    rows = BF // n
    odd = lax.axis_index("space") % 2
    copies = []
    for k in range(2 * n):
        at = pl.ds((k % n) * rows, rows)
        block, target = ((2 * odd, first_ref), (2 - 2 * odd, second_ref))[k // n]
        copies.append(
            (
                pltpu.make_async_copy(own_ref.at[block, at], held.at[k], sems.at[0, k]),
                pltpu.make_async_copy(held.at[k], target.at[0, at], sems.at[1, k]),
            )
        )
    for load, _ in copies:
        load.start()
    for load, store in copies:
        load.wait()
        store.start()
    for _, store in copies:
        store.wait()


def first_factors(own):
    return pl.pallas_call(
        first_kernel,
        out_shape=[jax.ShapeDtypeStruct((1, BF, COLS), jnp.bfloat16)] * 2,
        in_specs=[HBM],
        out_specs=[HBM] * 2,
        scratch_shapes=[
            pltpu.VMEM((8, BF // 4, COLS), jnp.bfloat16),
            pltpu.SemaphoreType.DMA((2, 8)),
        ],
        compiler_params=FAR,
        cost_estimate=pl.CostEstimate(flops=1 << 10, bytes_accessed=1 << 10, transcendentals=0),
    )(own)


def bring_kernel(ref, out_ref, sem):
    copy = pltpu.make_async_copy(ref, out_ref, sem)
    copy.start()
    copy.wait()


def bring(value):
    return pl.pallas_call(
        bring_kernel,
        out_shape=jax.ShapeDtypeStruct(value.shape, value.dtype),
        in_specs=[HBM],
        out_specs=VMEM,
        scratch_shapes=[pltpu.SemaphoreType.DMA],
        compiler_params=PARAMS,
        cost_estimate=pl.CostEstimate(flops=1 << 10, bytes_accessed=1 << 10, transcendentals=0),
    )(value)


def arrived_kernel(first_ref, second_ref, low_a_ref, low_b_ref, mine_ref, other_ref):
    place = here()

    def put(low_ref, high_ref):
        low_a_ref[0] = low_ref[0, :HALF, :]
        low_b_ref[0] = low_ref[0, HALF:, :]
        for core, target in ((place[0], mine_ref), (1 - place[0], other_ref)):
            for y in range(CHIPS):
                start = (2 * y + core) * SLICE
                target[0, y * SLICE : (y + 1) * SLICE, :] = high_ref[0, pl.ds(start, SLICE), :]

    @pl.when(place[2] == 1)
    def _():
        put(second_ref, first_ref)

    @pl.when(place[2] == 0)
    def _():
        put(first_ref, second_ref)


def arrived(first, second):
    return pl.pallas_call(
        arrived_kernel,
        out_shape=[jax.ShapeDtypeStruct((1, HALF, COLS), jnp.bfloat16)] * 4,
        in_specs=[VMEM, VMEM],
        out_specs=[VMEM] * 4,
        compiler_params=PARAMS,
        cost_estimate=pl.CostEstimate(flops=1 << 10, bytes_accessed=1 << 10, transcendentals=0),
    )(first, second)


def put_messages(place, refs, held):
    def put(refs):
        for ref, blocks in zip(refs, held):
            for k, (coded, _) in enumerate(blocks):
                ref[k * SLICE : (k + 1) * SLICE, :] = coded
            end = ref.shape[0] - 16
            ref[end : end + 16, :] = level_rows([level for _, level in blocks])

    if len(refs) < 2:
        put(refs)
        return

    @pl.when(place[2] == 1)
    def _():
        put(refs)

    @pl.when(place[2] == 0)
    def _():
        put(refs[::-1])


def add_kernel(places, first, sizes, keep, n_gots, lined, *refs):
    place = here()
    gots, refs = refs[:n_gots], refs[n_gots:]
    if n_gots == 1:
        gots = [gots[0].at[d] for d in range(CHIPS)]
    mask_ref, refs = refs[0], refs[1:]
    if lined:
        lines_ref, refs = refs[0], refs[1:]
    if keep:
        messages, sums = refs[: len(sizes)], refs[len(sizes)]
    else:
        if not first:
            refs = refs[2:]
        (f_ref, b_ref), refs = refs[:2], refs[2:]
        messages, (sums, sems) = refs[: len(sizes)], refs[len(sizes) :]
    held = [[] for _ in sizes]
    writes = []
    n = len(places)
    scales = [scales_of(gots[d][n * SLICE : n * SLICE + 16, :]) for d in range(CHIPS)]
    for p, ((theirs, block, slot), goals) in enumerate(places):
        total = None
        for d in range(CHIPS):
            part = gots[d][p * SLICE : (p + 1) * SLICE, :].astype(jnp.float32)
            part = part * scales[d][p : p + 1]
            total = part if total is None else total + part
        if theirs:
            line = lines_ref[block * 4 + slot : block * 4 + slot + 1, :]
            total = total * line
        else:
            total = total * mask_ref[block, slot].astype(jnp.float32)
        coded = None
        for kind, *goal in goals:
            if kind == "m":
                which, index = goal
                if coded is None:
                    (coded,), level = code([total])
                assert index == len(held[which])
                held[which].append((coded, level))
            elif kind == "kept":
                sums[goal[0]] = total
            else:
                sums[p] = total
                writes.append((p, (f_ref if kind == "f" else b_ref).at[goal[0], goal[1]]))
    put_messages(place, messages, held)
    writes = [
        pltpu.make_async_copy(sums.at[p], target, sems.at[k])
        for k, (p, target) in enumerate(writes)
    ]
    for copy in writes:
        copy.start()
    for copy in writes:
        copy.wait()


def add_parts(gots, masks, outs, places, sizes=(), kept=None):
    n = len(places)
    ins = [*gots, *masks]
    messages = [jax.ShapeDtypeStruct((coded_rows(max(sizes, default=0)), BF), jnp.int16)] * len(sizes)
    in_specs = [VMEM] * len(gots) + [SMEM, VMEM][: len(masks)]
    scratch, aliases = [], {}
    if kept is not None:
        shapes = messages + [jax.ShapeDtypeStruct((kept, SLICE, BF), jnp.float32)]
        out_specs = [VMEM] * len(shapes)
    else:
        shapes = OUTS + messages
        out_specs = [HBM] * 2 + [VMEM] * len(messages)
        scratch = [pltpu.VMEM((n, SLICE, BF), jnp.float32), pltpu.SemaphoreType.DMA((2 * n,))]
        if outs is not None:
            aliases = {len(ins): 0, len(ins) + 1: 1}
            ins += outs
            in_specs += [HBM] * 2
    kernel = functools.partial(
        add_kernel, places, outs is None, sizes, kept is not None, len(gots), len(masks) > 1
    )
    return pl.pallas_call(
        kernel,
        out_shape=shapes,
        in_specs=in_specs,
        out_specs=out_specs,
        scratch_shapes=scratch,
        input_output_aliases=aliases,
        compiler_params=PARAMS,
        cost_estimate=pl.CostEstimate(flops=1 << 20, bytes_accessed=1 << 16, transcendentals=0),
    )(*ins)


def place_kernel(below_places, above_places, block_places, n, first_ref, second_ref, *refs):
    blocks, refs = refs[:n], refs[n + 2 :]
    f_ref, b_ref, sums, sems = refs
    odd = here()[2] == 1
    end = first_ref.shape[0] - 16
    scales = [scales_of(ref[end : end + 16, :]) for ref in (first_ref, second_ref)]
    writes = []

    def write(source, goal):
        kind, block, slot = goal
        target = (f_ref if kind == "f" else b_ref).at[block, slot]
        writes.append(pltpu.make_async_copy(source, target, sems.at[len(writes)]))
        writes[-1].start()

    goals = iter(block_places)
    for ref in blocks:
        for source in [ref] if len(ref.shape) == 2 else [ref.at[k] for k in range(ref.shape[0])]:
            write(source, next(goals))
    k = 0
    for p in range(max(len(below_places), len(above_places))):
        rows = slice(p * SLICE, (p + 1) * SLICE)
        first, second = (
            ref[rows, :].astype(jnp.float32) * scale[p : p + 1]
            for ref, scale in zip((first_ref, second_ref), scales)
        )
        for places, values in ((below_places, (second, first)), (above_places, (first, second))):
            if p < len(places):
                sums[k] = jnp.where(odd, *values)
                write(sums.at[k], places[p])
                k += 1
    for copy in writes:
        copy.wait()


def place_results(first, second, outs, below_places, above_places, blocks=(), block_places=()):
    total = len(below_places) + len(above_places)
    n = 2 + len(blocks)
    return pl.pallas_call(
        functools.partial(place_kernel, below_places, above_places, block_places, len(blocks)),
        out_shape=OUTS,
        in_specs=[VMEM] * n + [HBM] * 2,
        out_specs=[HBM] * 2,
        scratch_shapes=[
            pltpu.VMEM((total, SLICE, BF), jnp.float32),
            pltpu.SemaphoreType.DMA((total + len(block_places),)),
        ],
        input_output_aliases={n: 0, n + 1: 1},
        compiler_params=PARAMS,
        cost_estimate=pl.CostEstimate(flops=1 << 20, bytes_accessed=1 << 16, transcendentals=0),
    )(first, second, *blocks, *outs)


def swap(value):
    return lax.ppermute(value, "occ", [(o, o ^ 1) for o in range(2 * CHIPS)])


def chips_on(value, by):
    pairs = [
        (2 * y + core, 2 * ((y + by) % CHIPS) + core) for y in range(CHIPS) for core in range(2)
    ]
    return lax.ppermute(value, "occ", pairs)


def across(value):
    groups = [[2 * y + core for y in range(CHIPS)] for core in range(2)]
    return lax.all_to_all(value, "occ", 0, 0, axis_index_groups=groups)


def to_chips(parts):
    return [parts[0]] + [chips_on(parts[d], d) for d in range(1, CHIPS)]


def pairwise(first, second):
    size = lax.axis_size("space")
    done = []
    for value, start in ((first, 1), (second, 0)):
        pairs = [(i, i + 1) for i in range(start, size - 1, 2)]
        pairs += [(j, i) for i, j in pairs]
        done.append(lax.ppermute(value, "space", sorted(pairs)))
    return done


def on_device(own, mask):
    own_sib = swap(own)
    first, second = pairwise(*first_factors(own))
    mine = {"own": own, "sib": own_sib}
    blocks = {k: ([("own", k)], [("sib", k)]) for k in range(3)}
    coded0, first2, second2 = pair_products(
        [(0, 1), (0, 2), (1, 2)], blocks, mine, together=True, mask=mask
    )
    first2, second2 = pairwise(first2, second2)
    got0 = [across(coded0)]
    first, second, got0 = lax.optimization_barrier((first, second, got0))
    low_a, low_b, high, other = arrived(first, second)
    low_as, low_bs, high_sib = swap((low_a, low_b, other))
    blocks["L"] = [("low_a", 0), ("low_b", 0)], [("low_as", 0), ("low_bs", 0)]
    blocks["H"] = [("high", 0)], [("high_sib", 0)]
    near, _ = lax.optimization_barrier((own_sib, low_a))
    coded1 = pair_products(
        [("L", 0), ("L", 1), ("L", 2), (0, "H"), (1, "H"), ("L", "H")],
        blocks,
        {"own": own, "sib": bring(near)}
        | {"low_a": low_a, "low_b": low_b, "low_as": low_as, "low_bs": low_bs}
        | {"high": high, "high_sib": high_sib},
    )
    got1 = to_chips(coded1)
    outs = add_parts(
        got0,
        [mask],
        None,
        [
            ((0, 0, 0), [("f", 0, 0), ("b", 1, 0)]),
            ((0, 0, 1), [("f", 0, 1), ("b", 2, 1)]),
            ((0, 1, 0), [("f", 1, 0), ("b", 2, 0)]),
        ],
    )
    near, _ = lax.optimization_barrier((own_sib, coded1[0]))
    near = bring(near)
    first2, second2, _, outs, near = lax.optimization_barrier((first2, second2, coded1[0], outs, near))
    blocks["H2"] = [("high2", 0)], [("high2", 1)]
    blocks["L2"] = [("low2", 0)], [("low2", 1)]
    *coded2, mine_half, other_half, lines = pair_products(
        [(0, "H2"), (1, "H2"), ("L2", 2)],
        blocks,
        {"own": own, "sib": near} | {"first": first2, "second": second2},
        halved=("L2",),
        late=True,
    )
    coded2 = whole(coded2, mine_half, swap(other_half))
    got2 = to_chips(coded2)
    *outs, up1, down1 = add_parts(
        got1,
        [mask, lines],
        outs,
        [
            ((1, 2, 0), [("b", 0, 0), ("m", 1, 0)]),
            ((1, 2, 1), [("b", 1, 1), ("m", 1, 1)]),
            ((1, 2, 2), [("b", 2, 2), ("m", 1, 2)]),
            ((0, 0, 2), [("f", 0, 2), ("m", 0, 0)]),
            ((0, 1, 1), [("f", 1, 1), ("m", 0, 1)]),
            ((1, 2, 3), [("m", 0, 2), ("m", 1, 3)]),
        ],
        (3, 4),
    )
    first3, second3 = pairwise(up1, down1)
    up2, down2, kept = add_parts(
        got2,
        [mask, lines],
        None,
        [
            ((0, 0, 3), [("kept", 0), ("m", 0, 0)]),
            ((0, 1, 2), [("kept", 1), ("m", 0, 1)]),
            ((1, 1, 3), [("kept", 2), ("m", 1, 0)]),
        ],
        (2, 1),
        kept=3,
    )
    first4, second4 = pairwise(up2, down2)
    outs = place_results(
        first3,
        second3,
        outs,
        [("b", 0, 2), ("b", 0, 1), ("b", 0, 3)],
        [("f", 2, 0), ("f", 2, 1), ("f", 2, 2), ("f", 2, 3)],
        [kept],
        [("f", 0, 3), ("f", 1, 2), ("b", 2, 3)],
    )
    forward, backward = place_results(
        first4, second4, outs, [("b", 1, 3), ("b", 1, 2)], [("f", 1, 3)]
    )
    return jnp.swapaxes(forward, 2, 3), backward


def solution(mesh):
    in_specs = (P("space", None, "occ"), P("space", None))
    out_specs = (P("space", None, None, "occ"), P("space", None, "occ", None))
    return jax.shard_map(
        on_device, mesh=mesh, in_specs=in_specs, out_specs=out_specs, check_vma=False
    )
```

```python
import functools

import jax
import jax.numpy as jnp
from jax import lax
from jax.experimental import pallas as pl
from jax.experimental.pallas import tpu as pltpu
from jax.sharding import PartitionSpec as P

BF = 512
COLS = 1024
HALF = 256
SLICE = 64
CHIPS = 4
AWAY = (0, 1, 3, 2)
STEPS = 256.0
TOP = 32700.0
LN2 = 0.6931471805599453

VMEM = pl.BlockSpec(memory_space=pltpu.VMEM)
SMEM = pl.BlockSpec(memory_space=pltpu.SMEM)
HBM = pl.BlockSpec(memory_space=pltpu.HBM)
PARAMS = pltpu.CompilerParams(vmem_limit_bytes=18 << 20)
FAR = pltpu.CompilerParams(vmem_limit_bytes=62 << 20)
OUTS = [jax.ShapeDtypeStruct((3, 4, SLICE, BF), jnp.float32)] * 2


def here():
    member = lax.axis_index("occ")
    return member & 1, member >> 1, lax.axis_index("space") & 1


def coded_rows(count):
    return count * SLICE + 16


def code(values):
    tops = jnp.concatenate([jnp.max(jnp.abs(v), 0, keepdims=True) for v in values], 0)
    level = jnp.ceil(jnp.log(jnp.maximum(tops, 1e-30) / TOP) * (STEPS / LN2))
    gain = jnp.exp(level * (-LN2 / STEPS))
    coded = [
        jnp.round(v * gain[i : i + 1]).astype(jnp.int32).astype(jnp.int16)
        for i, v in enumerate(values)
    ]
    return coded, level.astype(jnp.int32)


def level_rows(levels):
    rows = list(levels) + [jnp.zeros((16 - len(levels), BF), jnp.int32)]
    return jnp.concatenate(rows, 0).astype(jnp.int16)


def scales_of(rows):
    return jnp.exp(rows.astype(jnp.float32) * (LN2 / STEPS))


def pair_kernel(pairs, blocks, halved, names, together, late, with_second, *refs):
    place = here()
    ins = dict(zip(names, refs))
    outs = refs[len(names) :]
    if with_second:
        outs, mask_ref, second = outs[1:-2], outs[0], outs[-2:]
        put_second(place, mask_ref, (ins["own"], ins["sib"]), *second)
    if late:
        *outs, lines_ref = outs
        first_ref, second_ref = ins["first"], ins["second"]

        def work(low_ref, high_ref):
            ins.update({"low2": low_ref, "high2": high_ref})
            lines_ref[...] = low_ref[0, BF : BF + 16, :BF].astype(jnp.float32)
            pair_work(pairs, blocks, halved, ins, outs, together, place)

        @pl.when(place[2] == 1)
        def _():
            work(second_ref, first_ref)

        @pl.when(place[2] == 0)
        def _():
            work(first_ref, second_ref)

        return
    pair_work(pairs, blocks, halved, ins, outs, together, place)


def pair_work(pairs, blocks, halved, ins, outs, together, place):
    if together:
        outs = [outs[0].at[d] for d in range(CHIPS)]
    core, chip = place[0], place[1]
    stacked = ("low2", "high2")
    order = [d if together else (chip + AWAY[d]) % CHIPS for d in range(CHIPS)]

    def read(piece, start, rows):
        name, index = piece
        if name in stacked:
            return ins[name][0, pl.ds(index * HALF + start, rows), :]
        return ins[name][index, pl.ds(start, rows), :]

    def slices(pieces):
        rows = []
        for o in order:
            if len(pieces) == 2:
                start = (2 * (o % 2) + core) * SLICE
                low, high = (read(piece, start, SLICE) for piece in pieces)
                rows.append(jnp.where(o < 2, low, high))
            elif pieces[0][0] in stacked or ins[pieces[0][0]].shape[1] < BF:
                rows.append(read(pieces[0], o * SLICE, SLICE))
            else:
                rows.append(read(pieces[0], (2 * o + core) * SLICE, SLICE))
        return jnp.concatenate(rows, 0)

    def both_slices(pieces):
        rows = [read(pieces[0], o * 2 * SLICE, 2 * SLICE) for o in order]
        return jnp.concatenate(rows, 0)

    def term(a, b, part):
        shared = a in halved
        right = (both_slices if shared else slices)(blocks[b][part])
        pieces = blocks[a][part]
        rows = (HALF if shared else BF) // len(pieces)
        values = [
            lax.dot_general(
                right,
                read(piece, 0, rows),
                (((1,), (1,)), ((), ())),
                preferred_element_type=jnp.float32,
            )
            for piece in pieces
        ]
        return jnp.concatenate(values, 1)

    levels = []
    for p, (a, b) in enumerate(pairs):
        shared = a in halved
        acc = term(a, b, 0) + term(a, b, 1)
        if shared:
            parts = [
                jnp.concatenate(
                    [acc[k * SLICE : (k + 1) * SLICE] for k in (2 * d, 2 * d + 1)], 1
                )
                for d in range(CHIPS)
            ]
        else:
            parts = [acc[d * SLICE : (d + 1) * SLICE] for d in range(CHIPS)]
        coded, level = code(parts)
        if shared:
            for k in range(2):

                @pl.when(core == k)
                def _():
                    for d in range(CHIPS):
                        row = level_rows([level[d : d + 1]])
                        for ref, j in zip(outs[CHIPS:], (k, 1 - k)):
                            lanes = slice(j * HALF, (j + 1) * HALF)
                            ref[d, :SLICE, :] = coded[d][:, lanes]
                            ref[d, SLICE:, :] = row[:, lanes]

            continue
        for d in range(CHIPS):
            outs[d][p * SLICE : (p + 1) * SLICE, :] = coded[d]
        levels.append(level)
    end = len(levels) * SLICE
    for d in range(CHIPS):
        outs[d][end : end + 16, :] = level_rows([v[d : d + 1] for v in levels])


def put_second(place, mask_ref, sources, first_ref, second_ref):
    core = place[0]
    lines = [
        jnp.full((1, COLS), mask_ref[k // 4, k % 4].astype(jnp.float32), jnp.float32)
        for k in range(12)
    ]
    lines.append(jnp.zeros((4, COLS), jnp.float32))
    lines = jnp.concatenate(lines, 0).astype(jnp.bfloat16)

    def put(up_ref, down_ref):
        for i, source in enumerate(sources):
            up_ref[0, i * HALF : (i + 1) * HALF, :] = source[1, pl.ds(core * HALF, HALF), :]
            for y in range(CHIPS):
                row = i * HALF + y * SLICE
                down_ref[0, row : row + SLICE, :] = source[
                    1, pl.ds((2 * y + core) * SLICE, SLICE), :
                ]
        up_ref[0, BF:, :] = lines
        down_ref[0, BF:, :] = lines

    @pl.when(place[2] == 1)
    def _():
        put(first_ref, second_ref)

    @pl.when(place[2] == 0)
    def _():
        put(second_ref, first_ref)


def pair_products(pairs, blocks, operands, halved=(), together=False, late=False, mask=None):
    names = list(operands)
    rows = coded_rows(len(pairs) - len(halved))
    shapes = [jax.ShapeDtypeStruct((rows, BF), jnp.int16)] * CHIPS
    if together:
        shapes = [jax.ShapeDtypeStruct((CHIPS, rows, BF), jnp.int16)]
    if halved:
        shapes += [jax.ShapeDtypeStruct((CHIPS, SLICE + 16, HALF), jnp.int16)] * 2
    if late:
        shapes.append(jax.ShapeDtypeStruct((16, BF), jnp.float32))
    second = mask is not None
    if second:
        shapes += [jax.ShapeDtypeStruct((1, BF + 16, COLS), jnp.bfloat16)] * 2
    return pl.pallas_call(
        functools.partial(pair_kernel, pairs, blocks, halved, names, together, late, second),
        out_shape=shapes,
        in_specs=[VMEM] * len(names) + [SMEM] * second,
        out_specs=[VMEM] * len(shapes),
        compiler_params=FAR if together else PARAMS,
        cost_estimate=pl.CostEstimate(flops=1 << 20, bytes_accessed=1 << 16, transcendentals=0),
    )(*operands.values(), *([mask] if second else []))


def whole_kernel(*refs):
    place = here()
    coded, (mine_ref, other_ref), outs = refs[:CHIPS], refs[CHIPS : CHIPS + 2], refs[CHIPS + 2 :]
    for d in range(CHIPS):
        end = coded[d].shape[0] - 16
        outs[d][:end, :] = coded[d][:end, :]
        levels = coded[d][end : end + 16, :].astype(jnp.int32)
        for k in range(2):

            @pl.when(place[0] == k)
            def _():
                refs = (mine_ref, other_ref) if k == 0 else (other_ref, mine_ref)
                block = jnp.concatenate([ref[d, :SLICE, :] for ref in refs], 1)
                outs[d][end : end + SLICE, :] = block
                row = [ref[d, SLICE:, :].astype(jnp.int32)[:1] for ref in refs]
                rows = [levels[i : i + 1] for i in range(end // SLICE)]
                rows.append(jnp.concatenate(row, 1))
                outs[d][end + SLICE :, :] = level_rows(rows)


def whole(coded, mine, other):
    rows = coded[0].shape[0] + SLICE
    return pl.pallas_call(
        whole_kernel,
        out_shape=[jax.ShapeDtypeStruct((rows, BF), jnp.int16)] * CHIPS,
        in_specs=[VMEM] * (CHIPS + 2),
        out_specs=[VMEM] * CHIPS,
        compiler_params=PARAMS,
        cost_estimate=pl.CostEstimate(flops=1 << 10, bytes_accessed=1 << 10, transcendentals=0),
    )(*coded, mine, other)


def first_kernel(own_ref, first_ref, second_ref, held, sems):
    n = 4
    rows = BF // n
    odd = lax.axis_index("space") % 2
    copies = []
    for k in range(2 * n):
        at = pl.ds((k % n) * rows, rows)
        block, target = ((2 * odd, first_ref), (2 - 2 * odd, second_ref))[k // n]
        copies.append(
            (
                pltpu.make_async_copy(own_ref.at[block, at], held.at[k], sems.at[0, k]),
                pltpu.make_async_copy(held.at[k], target.at[0, at], sems.at[1, k]),
            )
        )
    for load, _ in copies:
        load.start()
    for load, store in copies:
        load.wait()
        store.start()
    for _, store in copies:
        store.wait()


def first_factors(own):
    return pl.pallas_call(
        first_kernel,
        out_shape=[jax.ShapeDtypeStruct((1, BF, COLS), jnp.bfloat16)] * 2,
        in_specs=[HBM],
        out_specs=[HBM] * 2,
        scratch_shapes=[
            pltpu.VMEM((8, BF // 4, COLS), jnp.bfloat16),
            pltpu.SemaphoreType.DMA((2, 8)),
        ],
        compiler_params=FAR,
        cost_estimate=pl.CostEstimate(flops=1 << 10, bytes_accessed=1 << 10, transcendentals=0),
    )(own)


def bring_kernel(ref, out_ref, sem):
    copy = pltpu.make_async_copy(ref, out_ref, sem)
    copy.start()
    copy.wait()


def bring(value):
    return pl.pallas_call(
        bring_kernel,
        out_shape=jax.ShapeDtypeStruct(value.shape, value.dtype),
        in_specs=[HBM],
        out_specs=VMEM,
        scratch_shapes=[pltpu.SemaphoreType.DMA],
        compiler_params=PARAMS,
        cost_estimate=pl.CostEstimate(flops=1 << 10, bytes_accessed=1 << 10, transcendentals=0),
    )(value)


def arrived_kernel(first_ref, second_ref, low_a_ref, low_b_ref, mine_ref, other_ref):
    place = here()

    def put(low_ref, high_ref):
        low_a_ref[0] = low_ref[0, :HALF, :]
        low_b_ref[0] = low_ref[0, HALF:, :]
        for core, target in ((place[0], mine_ref), (1 - place[0], other_ref)):
            for y in range(CHIPS):
                start = (2 * y + core) * SLICE
                target[0, y * SLICE : (y + 1) * SLICE, :] = high_ref[0, pl.ds(start, SLICE), :]

    @pl.when(place[2] == 1)
    def _():
        put(second_ref, first_ref)

    @pl.when(place[2] == 0)
    def _():
        put(first_ref, second_ref)


def arrived(first, second):
    return pl.pallas_call(
        arrived_kernel,
        out_shape=[jax.ShapeDtypeStruct((1, HALF, COLS), jnp.bfloat16)] * 4,
        in_specs=[VMEM, VMEM],
        out_specs=[VMEM] * 4,
        compiler_params=PARAMS,
        cost_estimate=pl.CostEstimate(flops=1 << 10, bytes_accessed=1 << 10, transcendentals=0),
    )(first, second)


def put_messages(place, refs, held):
    def put(refs):
        for ref, blocks in zip(refs, held):
            for k, (coded, _) in enumerate(blocks):
                ref[k * SLICE : (k + 1) * SLICE, :] = coded
            end = ref.shape[0] - 16
            ref[end : end + 16, :] = level_rows([level for _, level in blocks])

    if len(refs) < 2:
        put(refs)
        return

    @pl.when(place[2] == 1)
    def _():
        put(refs)

    @pl.when(place[2] == 0)
    def _():
        put(refs[::-1])


def add_kernel(places, first, sizes, keep, n_gots, lined, *refs):
    place = here()
    gots, refs = refs[:n_gots], refs[n_gots:]
    if n_gots == 1:
        gots = [gots[0].at[d] for d in range(CHIPS)]
    mask_ref, refs = refs[0], refs[1:]
    if lined:
        lines_ref, refs = refs[0], refs[1:]
    if keep:
        messages, sums = refs[: len(sizes)], refs[len(sizes)]
    else:
        if not first:
            refs = refs[2:]
        (f_ref, b_ref), refs = refs[:2], refs[2:]
        messages, (sums, sems) = refs[: len(sizes)], refs[len(sizes) :]
    held = [[] for _ in sizes]
    writes = []
    n = len(places)
    scales = [scales_of(gots[d][n * SLICE : n * SLICE + 16, :]) for d in range(CHIPS)]
    for p, ((theirs, block, slot), goals) in enumerate(places):
        total = None
        for d in range(CHIPS):
            part = gots[d][p * SLICE : (p + 1) * SLICE, :].astype(jnp.float32)
            part = part * scales[d][p : p + 1]
            total = part if total is None else total + part
        if theirs:
            line = lines_ref[block * 4 + slot : block * 4 + slot + 1, :]
            total = total * line
        else:
            total = total * mask_ref[block, slot].astype(jnp.float32)
        coded = None
        for kind, *goal in goals:
            if kind == "m":
                which, index = goal
                if coded is None:
                    (coded,), level = code([total])
                assert index == len(held[which])
                held[which].append((coded, level))
            elif kind == "kept":
                sums[goal[0]] = total
            else:
                sums[p] = total
                writes.append((p, (f_ref if kind == "f" else b_ref).at[goal[0], goal[1]]))
    put_messages(place, messages, held)
    writes = [
        pltpu.make_async_copy(sums.at[p], target, sems.at[k])
        for k, (p, target) in enumerate(writes)
    ]
    for copy in writes:
        copy.start()
    for copy in writes:
        copy.wait()


def add_parts(gots, masks, outs, places, sizes=(), kept=None):
    n = len(places)
    ins = [*gots, *masks]
    messages = [jax.ShapeDtypeStruct((coded_rows(max(sizes, default=0)), BF), jnp.int16)] * len(sizes)
    in_specs = [VMEM] * len(gots) + [SMEM, VMEM][: len(masks)]
    scratch, aliases = [], {}
    if kept is not None:
        shapes = messages + [jax.ShapeDtypeStruct((kept, SLICE, BF), jnp.float32)]
        out_specs = [VMEM] * len(shapes)
    else:
        shapes = OUTS + messages
        out_specs = [HBM] * 2 + [VMEM] * len(messages)
        scratch = [pltpu.VMEM((n, SLICE, BF), jnp.float32), pltpu.SemaphoreType.DMA((2 * n,))]
        if outs is not None:
            aliases = {len(ins): 0, len(ins) + 1: 1}
            ins += outs
            in_specs += [HBM] * 2
    kernel = functools.partial(
        add_kernel, places, outs is None, sizes, kept is not None, len(gots), len(masks) > 1
    )
    return pl.pallas_call(
        kernel,
        out_shape=shapes,
        in_specs=in_specs,
        out_specs=out_specs,
        scratch_shapes=scratch,
        input_output_aliases=aliases,
        compiler_params=PARAMS,
        cost_estimate=pl.CostEstimate(flops=1 << 20, bytes_accessed=1 << 16, transcendentals=0),
    )(*ins)


def place_kernel(below_places, above_places, block_places, n, first_ref, second_ref, *refs):
    blocks, refs = refs[:n], refs[n + 2 :]
    f_ref, b_ref, sums, sems = refs
    odd = here()[2] == 1
    end = first_ref.shape[0] - 16
    scales = [scales_of(ref[end : end + 16, :]) for ref in (first_ref, second_ref)]
    writes = []

    def write(source, goal):
        kind, block, slot = goal
        target = (f_ref if kind == "f" else b_ref).at[block, slot]
        writes.append(pltpu.make_async_copy(source, target, sems.at[len(writes)]))
        writes[-1].start()

    goals = iter(block_places)
    for ref in blocks:
        for source in [ref] if len(ref.shape) == 2 else [ref.at[k] for k in range(ref.shape[0])]:
            write(source, next(goals))
    k = 0
    for p in range(max(len(below_places), len(above_places))):
        rows = slice(p * SLICE, (p + 1) * SLICE)
        first, second = (
            ref[rows, :].astype(jnp.float32) * scale[p : p + 1]
            for ref, scale in zip((first_ref, second_ref), scales)
        )
        for places, values in ((below_places, (second, first)), (above_places, (first, second))):
            if p < len(places):
                sums[k] = jnp.where(odd, *values)
                write(sums.at[k], places[p])
                k += 1
    for copy in writes:
        copy.wait()


def place_results(first, second, outs, below_places, above_places, blocks=(), block_places=()):
    total = len(below_places) + len(above_places)
    n = 2 + len(blocks)
    return pl.pallas_call(
        functools.partial(place_kernel, below_places, above_places, block_places, len(blocks)),
        out_shape=OUTS,
        in_specs=[VMEM] * n + [HBM] * 2,
        out_specs=[HBM] * 2,
        scratch_shapes=[
            pltpu.VMEM((total, SLICE, BF), jnp.float32),
            pltpu.SemaphoreType.DMA((total + len(block_places),)),
        ],
        input_output_aliases={n: 0, n + 1: 1},
        compiler_params=PARAMS,
        cost_estimate=pl.CostEstimate(flops=1 << 20, bytes_accessed=1 << 16, transcendentals=0),
    )(first, second, *blocks, *outs)


def swap(value):
    return lax.ppermute(value, "occ", [(o, o ^ 1) for o in range(2 * CHIPS)])


def chips_on(value, by):
    pairs = [
        (2 * y + core, 2 * ((y + by) % CHIPS) + core) for y in range(CHIPS) for core in range(2)
    ]
    return lax.ppermute(value, "occ", pairs)


def across(value):
    groups = [[2 * y + core for y in range(CHIPS)] for core in range(2)]
    return lax.all_to_all(value, "occ", 0, 0, axis_index_groups=groups)


def to_chips(parts):
    return [parts[0]] + [chips_on(parts[d], AWAY[d]) for d in range(1, CHIPS)]


def pairwise(first, second):
    size = lax.axis_size("space")
    done = []
    for value, start in ((first, 1), (second, 0)):
        pairs = [(i, i + 1) for i in range(start, size - 1, 2)]
        pairs += [(j, i) for i, j in pairs]
        done.append(lax.ppermute(value, "space", sorted(pairs)))
    return done


def on_device(own, mask):
    own_sib = swap(own)
    first, second = pairwise(*first_factors(own))
    mine = {"own": own, "sib": own_sib}
    blocks = {k: ([("own", k)], [("sib", k)]) for k in range(3)}
    coded0, first2, second2 = pair_products(
        [(0, 1), (0, 2), (1, 2)], blocks, mine, together=True, mask=mask
    )
    first2, second2 = pairwise(first2, second2)
    got0 = [across(coded0)]
    first, second, got0 = lax.optimization_barrier((first, second, got0))
    low_a, low_b, high, other = arrived(first, second)
    low_as, low_bs, high_sib = swap((low_a, low_b, other))
    blocks["L"] = [("low_a", 0), ("low_b", 0)], [("low_as", 0), ("low_bs", 0)]
    blocks["H"] = [("high", 0)], [("high_sib", 0)]
    near, _ = lax.optimization_barrier((own_sib, low_a))
    coded1 = pair_products(
        [("L", 0), ("L", 1), ("L", 2), (0, "H"), (1, "H"), ("L", "H")],
        blocks,
        {"own": own, "sib": bring(near)}
        | {"low_a": low_a, "low_b": low_b, "low_as": low_as, "low_bs": low_bs}
        | {"high": high, "high_sib": high_sib},
    )
    got1 = to_chips(coded1)
    outs = add_parts(
        got0,
        [mask],
        None,
        [
            ((0, 0, 0), [("f", 0, 0), ("b", 1, 0)]),
            ((0, 0, 1), [("f", 0, 1), ("b", 2, 1)]),
            ((0, 1, 0), [("f", 1, 0), ("b", 2, 0)]),
        ],
    )
    near, _ = lax.optimization_barrier((own_sib, coded1[0]))
    near = bring(near)
    first2, second2, _, outs, near = lax.optimization_barrier((first2, second2, coded1[0], outs, near))
    blocks["H2"] = [("high2", 0)], [("high2", 1)]
    blocks["L2"] = [("low2", 0)], [("low2", 1)]
    *coded2, mine_half, other_half, lines = pair_products(
        [(0, "H2"), (1, "H2"), ("L2", 2)],
        blocks,
        {"own": own, "sib": near} | {"first": first2, "second": second2},
        halved=("L2",),
        late=True,
    )
    coded2 = whole(coded2, mine_half, swap(other_half))
    got2 = to_chips(coded2)
    *outs, up1, down1 = add_parts(
        got1,
        [mask, lines],
        outs,
        [
            ((1, 2, 0), [("b", 0, 0), ("m", 1, 0)]),
            ((1, 2, 1), [("b", 1, 1), ("m", 1, 1)]),
            ((1, 2, 2), [("b", 2, 2), ("m", 1, 2)]),
            ((0, 0, 2), [("f", 0, 2), ("m", 0, 0)]),
            ((0, 1, 1), [("f", 1, 1), ("m", 0, 1)]),
            ((1, 2, 3), [("m", 0, 2), ("m", 1, 3)]),
        ],
        (3, 4),
    )
    first3, second3 = pairwise(up1, down1)
    up2, down2, kept = add_parts(
        got2,
        [mask, lines],
        None,
        [
            ((0, 0, 3), [("kept", 0), ("m", 0, 0)]),
            ((0, 1, 2), [("kept", 1), ("m", 0, 1)]),
            ((1, 1, 3), [("kept", 2), ("m", 1, 0)]),
        ],
        (2, 1),
        kept=3,
    )
    first4, second4 = pairwise(up2, down2)
    outs = place_results(
        first3,
        second3,
        outs,
        [("b", 0, 2), ("b", 0, 1), ("b", 0, 3)],
        [("f", 2, 0), ("f", 2, 1), ("f", 2, 2), ("f", 2, 3)],
        [kept],
        [("f", 0, 3), ("f", 1, 2), ("b", 2, 3)],
    )
    forward, backward = place_results(
        first4, second4, outs, [("b", 1, 3), ("b", 1, 2)], [("f", 1, 3)]
    )
    return jnp.swapaxes(forward, 2, 3), backward


def solution(mesh):
    in_specs = (P("space", None, "occ"), P("space", None))
    out_specs = (P("space", None, None, "occ"), P("space", None, "occ", None))
    return jax.shard_map(
        on_device, mesh=mesh, in_specs=in_specs, out_specs=out_specs, check_vma=False
    )
```

```python
import functools

import jax
import jax.numpy as jnp
from jax import lax
from jax.experimental import pallas as pl
from jax.experimental.pallas import tpu as pltpu
from jax.sharding import PartitionSpec as P

BF = 512
COLS = 1024
HALF = 256
SLICE = 64
CHIPS = 4
AWAY = (0, 1, 3, 2)
STEPS = 256.0
TOP = 32700.0
LN2 = 0.6931471805599453

VMEM = pl.BlockSpec(memory_space=pltpu.VMEM)
SMEM = pl.BlockSpec(memory_space=pltpu.SMEM)
HBM = pl.BlockSpec(memory_space=pltpu.HBM)
PARAMS = pltpu.CompilerParams(vmem_limit_bytes=18 << 20)
FAR = pltpu.CompilerParams(vmem_limit_bytes=62 << 20)
OUTS = [jax.ShapeDtypeStruct((3, 4, SLICE, BF), jnp.float32)] * 2


def here():
    member = lax.axis_index("occ")
    return member & 1, member >> 1, lax.axis_index("space") & 1


def coded_rows(count):
    return count * SLICE + 16


def code(values):
    tops = jnp.concatenate([jnp.max(jnp.abs(v), 0, keepdims=True) for v in values], 0)
    level = jnp.ceil(jnp.log(jnp.maximum(tops, 1e-30) / TOP) * (STEPS / LN2))
    gain = jnp.exp(level * (-LN2 / STEPS))
    coded = [
        jnp.round(v * gain[i : i + 1]).astype(jnp.int32).astype(jnp.int16)
        for i, v in enumerate(values)
    ]
    return coded, level.astype(jnp.int32)


def level_rows(levels):
    rows = list(levels) + [jnp.zeros((16 - len(levels), BF), jnp.int32)]
    return jnp.concatenate(rows, 0).astype(jnp.int16)


def scales_of(rows):
    return jnp.exp(rows.astype(jnp.float32) * (LN2 / STEPS))


def pair_kernel(pairs, blocks, halved, names, together, late, with_second, *refs):
    place = here()
    ins = dict(zip(names, refs))
    outs = refs[len(names) :]
    if with_second:
        outs, mask_ref, second = outs[1:-2], outs[0], outs[-2:]
        put_second(place, mask_ref, (ins["own"], ins["sib"]), *second)
    if late:
        *outs, lines_ref = outs
        first_ref, second_ref = ins["first"], ins["second"]

        def work(low_ref, high_ref):
            ins.update({"low2": low_ref, "high2": high_ref})
            lines_ref[...] = low_ref[0, BF : BF + 16, :BF].astype(jnp.float32)
            pair_work(pairs, blocks, halved, ins, outs, together, place)

        @pl.when(place[2] == 1)
        def _():
            work(second_ref, first_ref)

        @pl.when(place[2] == 0)
        def _():
            work(first_ref, second_ref)

        return
    pair_work(pairs, blocks, halved, ins, outs, together, place)


def pair_work(pairs, blocks, halved, ins, outs, together, place):
    if together:
        outs = [outs[0].at[d] for d in range(CHIPS)]
    core, chip = place[0], place[1]
    stacked = ("low2", "high2")
    order = [d if together else (chip + AWAY[d]) % CHIPS for d in range(CHIPS)]

    def read(piece, start, rows):
        name, index = piece
        if name in stacked:
            return ins[name][0, pl.ds(index * HALF + start, rows), :]
        return ins[name][index, pl.ds(start, rows), :]

    def slices(pieces):
        rows = []
        for o in order:
            if len(pieces) == 2:
                start = (2 * (o % 2) + core) * SLICE
                low, high = (read(piece, start, SLICE) for piece in pieces)
                rows.append(jnp.where(o < 2, low, high))
            elif pieces[0][0] in stacked or ins[pieces[0][0]].shape[1] < BF:
                rows.append(read(pieces[0], o * SLICE, SLICE))
            else:
                rows.append(read(pieces[0], (2 * o + core) * SLICE, SLICE))
        return jnp.concatenate(rows, 0)

    def both_slices(pieces):
        rows = [read(pieces[0], o * 2 * SLICE, 2 * SLICE) for o in order]
        return jnp.concatenate(rows, 0)

    def term(a, b, part):
        shared = a in halved
        right = (both_slices if shared else slices)(blocks[b][part])
        pieces = blocks[a][part]
        rows = (HALF if shared else BF) // len(pieces)
        values = [
            lax.dot_general(
                right,
                read(piece, 0, rows),
                (((1,), (1,)), ((), ())),
                preferred_element_type=jnp.float32,
            )
            for piece in pieces
        ]
        return jnp.concatenate(values, 1)

    levels = []
    for p, (a, b) in enumerate(pairs):
        shared = a in halved
        acc = term(a, b, 0) + term(a, b, 1)
        if shared:
            parts = [
                jnp.concatenate(
                    [acc[k * SLICE : (k + 1) * SLICE] for k in (2 * d, 2 * d + 1)], 1
                )
                for d in range(CHIPS)
            ]
        else:
            parts = [acc[d * SLICE : (d + 1) * SLICE] for d in range(CHIPS)]
        coded, level = code(parts)
        if shared:
            for k in range(2):

                @pl.when(core == k)
                def _():
                    for d in range(CHIPS):
                        row = level_rows([level[d : d + 1]])
                        for ref, j in zip(outs[CHIPS:], (k, 1 - k)):
                            lanes = slice(j * HALF, (j + 1) * HALF)
                            ref[d, :SLICE, :] = coded[d][:, lanes]
                            ref[d, SLICE:, :] = row[:, lanes]

            continue
        for d in range(CHIPS):
            outs[d][p * SLICE : (p + 1) * SLICE, :] = coded[d]
        levels.append(level)
    end = len(levels) * SLICE
    for d in range(CHIPS):
        outs[d][end : end + 16, :] = level_rows([v[d : d + 1] for v in levels])


def put_second(place, mask_ref, sources, first_ref, second_ref):
    core = place[0]
    lines = [
        jnp.full((1, COLS), mask_ref[k // 4, k % 4].astype(jnp.float32), jnp.float32)
        for k in range(12)
    ]
    lines.append(jnp.zeros((4, COLS), jnp.float32))
    lines = jnp.concatenate(lines, 0).astype(jnp.bfloat16)

    def put(up_ref, down_ref):
        for i, source in enumerate(sources):
            up_ref[0, i * HALF : (i + 1) * HALF, :] = source[1, pl.ds(core * HALF, HALF), :]
            for y in range(CHIPS):
                row = i * HALF + y * SLICE
                down_ref[0, row : row + SLICE, :] = source[
                    1, pl.ds((2 * y + core) * SLICE, SLICE), :
                ]
        up_ref[0, BF:, :] = lines
        down_ref[0, BF:, :] = lines

    @pl.when(place[2] == 1)
    def _():
        put(first_ref, second_ref)

    @pl.when(place[2] == 0)
    def _():
        put(second_ref, first_ref)


def pair_products(pairs, blocks, operands, halved=(), together=False, late=False, mask=None):
    names = list(operands)
    rows = coded_rows(len(pairs) - len(halved))
    shapes = [jax.ShapeDtypeStruct((rows, BF), jnp.int16)] * CHIPS
    if together:
        shapes = [jax.ShapeDtypeStruct((CHIPS, rows, BF), jnp.int16)]
    if halved:
        shapes += [jax.ShapeDtypeStruct((CHIPS, SLICE + 16, HALF), jnp.int16)] * 2
    if late:
        shapes.append(jax.ShapeDtypeStruct((16, BF), jnp.float32))
    second = mask is not None
    if second:
        shapes += [jax.ShapeDtypeStruct((1, BF + 16, COLS), jnp.bfloat16)] * 2
    return pl.pallas_call(
        functools.partial(pair_kernel, pairs, blocks, halved, names, together, late, second),
        out_shape=shapes,
        in_specs=[VMEM] * len(names) + [SMEM] * second,
        out_specs=[VMEM] * len(shapes),
        compiler_params=FAR if together else PARAMS,
        cost_estimate=pl.CostEstimate(flops=1 << 20, bytes_accessed=1 << 16, transcendentals=0),
    )(*operands.values(), *([mask] if second else []))


def whole_kernel(*refs):
    place = here()
    coded, (mine_ref, other_ref), outs = refs[:CHIPS], refs[CHIPS : CHIPS + 2], refs[CHIPS + 2 :]
    for d in range(CHIPS):
        end = coded[d].shape[0] - 16
        outs[d][:end, :] = coded[d][:end, :]
        levels = coded[d][end : end + 16, :].astype(jnp.int32)
        for k in range(2):

            @pl.when(place[0] == k)
            def _():
                refs = (mine_ref, other_ref) if k == 0 else (other_ref, mine_ref)
                block = jnp.concatenate([ref[d, :SLICE, :] for ref in refs], 1)
                outs[d][end : end + SLICE, :] = block
                row = [ref[d, SLICE:, :].astype(jnp.int32)[:1] for ref in refs]
                rows = [levels[i : i + 1] for i in range(end // SLICE)]
                rows.append(jnp.concatenate(row, 1))
                outs[d][end + SLICE :, :] = level_rows(rows)


def whole(coded, mine, other):
    rows = coded[0].shape[0] + SLICE
    return pl.pallas_call(
        whole_kernel,
        out_shape=[jax.ShapeDtypeStruct((rows, BF), jnp.int16)] * CHIPS,
        in_specs=[VMEM] * (CHIPS + 2),
        out_specs=[VMEM] * CHIPS,
        compiler_params=PARAMS,
        cost_estimate=pl.CostEstimate(flops=1 << 10, bytes_accessed=1 << 10, transcendentals=0),
    )(*coded, mine, other)


def first_kernel(own_ref, first_ref, second_ref, held, sems):
    n = 4
    rows = BF // n
    odd = lax.axis_index("space") % 2
    copies = []
    for k in range(2 * n):
        at = pl.ds((k % n) * rows, rows)
        block, target = ((2 * odd, first_ref), (2 - 2 * odd, second_ref))[k // n]
        copies.append(
            (
                pltpu.make_async_copy(own_ref.at[block, at], held.at[k], sems.at[0, k]),
                pltpu.make_async_copy(held.at[k], target.at[0, at], sems.at[1, k]),
            )
        )
    for load, _ in copies:
        load.start()
    for load, store in copies:
        load.wait()
        store.start()
    for _, store in copies:
        store.wait()


def first_factors(own):
    return pl.pallas_call(
        first_kernel,
        out_shape=[jax.ShapeDtypeStruct((1, BF, COLS), jnp.bfloat16)] * 2,
        in_specs=[HBM],
        out_specs=[HBM] * 2,
        scratch_shapes=[
            pltpu.VMEM((8, BF // 4, COLS), jnp.bfloat16),
            pltpu.SemaphoreType.DMA((2, 8)),
        ],
        compiler_params=FAR,
        cost_estimate=pl.CostEstimate(flops=1 << 10, bytes_accessed=1 << 10, transcendentals=0),
    )(own)


def bring_kernel(ref, out_ref, sem):
    copy = pltpu.make_async_copy(ref, out_ref, sem)
    copy.start()
    copy.wait()


def bring(value):
    return pl.pallas_call(
        bring_kernel,
        out_shape=jax.ShapeDtypeStruct(value.shape, value.dtype),
        in_specs=[HBM],
        out_specs=VMEM,
        scratch_shapes=[pltpu.SemaphoreType.DMA],
        compiler_params=PARAMS,
        cost_estimate=pl.CostEstimate(flops=1 << 10, bytes_accessed=1 << 10, transcendentals=0),
    )(value)


def arrived_kernel(first_ref, second_ref, low_a_ref, low_b_ref, mine_ref, other_ref):
    place = here()

    def put(low_ref, high_ref):
        low_a_ref[0] = low_ref[0, :HALF, :]
        low_b_ref[0] = low_ref[0, HALF:, :]
        for core, target in ((place[0], mine_ref), (1 - place[0], other_ref)):
            for y in range(CHIPS):
                start = (2 * y + core) * SLICE
                target[0, y * SLICE : (y + 1) * SLICE, :] = high_ref[0, pl.ds(start, SLICE), :]

    @pl.when(place[2] == 1)
    def _():
        put(second_ref, first_ref)

    @pl.when(place[2] == 0)
    def _():
        put(first_ref, second_ref)


def arrived(first, second):
    return pl.pallas_call(
        arrived_kernel,
        out_shape=[jax.ShapeDtypeStruct((1, HALF, COLS), jnp.bfloat16)] * 4,
        in_specs=[VMEM, VMEM],
        out_specs=[VMEM] * 4,
        compiler_params=PARAMS,
        cost_estimate=pl.CostEstimate(flops=1 << 10, bytes_accessed=1 << 10, transcendentals=0),
    )(first, second)


def put_messages(place, refs, held):
    def put(refs):
        for ref, blocks in zip(refs, held):
            for k, (coded, _) in enumerate(blocks):
                ref[k * SLICE : (k + 1) * SLICE, :] = coded
            end = ref.shape[0] - 16
            ref[end : end + 16, :] = level_rows([level for _, level in blocks])

    if len(refs) < 2:
        put(refs)
        return

    @pl.when(place[2] == 1)
    def _():
        put(refs)

    @pl.when(place[2] == 0)
    def _():
        put(refs[::-1])


def add_kernel(places, first, sizes, keep, n_gots, lined, *refs):
    place = here()
    gots, refs = refs[:n_gots], refs[n_gots:]
    if n_gots == 1:
        gots = [gots[0].at[d] for d in range(CHIPS)]
    mask_ref, refs = refs[0], refs[1:]
    if lined:
        lines_ref, refs = refs[0], refs[1:]
    if keep:
        messages, sums = refs[: len(sizes)], refs[len(sizes)]
    else:
        if not first:
            refs = refs[2:]
        (f_ref, b_ref), refs = refs[:2], refs[2:]
        messages, (sums, sems) = refs[: len(sizes)], refs[len(sizes) :]
    held = [[] for _ in sizes]
    writes = []
    n = len(places)
    scales = [scales_of(gots[d][n * SLICE : n * SLICE + 16, :]) for d in range(CHIPS)]
    for p, ((theirs, block, slot), goals) in enumerate(places):
        total = None
        for d in range(CHIPS):
            part = gots[d][p * SLICE : (p + 1) * SLICE, :].astype(jnp.float32)
            part = part * scales[d][p : p + 1]
            total = part if total is None else total + part
        if theirs:
            line = lines_ref[block * 4 + slot : block * 4 + slot + 1, :]
            total = total * line
        else:
            total = total * mask_ref[block, slot].astype(jnp.float32)
        coded = None
        for kind, *goal in goals:
            if kind == "m":
                which, index = goal
                if coded is None:
                    (coded,), level = code([total])
                assert index == len(held[which])
                held[which].append((coded, level))
            elif kind == "kept":
                sums[goal[0]] = total
            else:
                sums[p] = total
                writes.append((p, (f_ref if kind == "f" else b_ref).at[goal[0], goal[1]]))
    put_messages(place, messages, held)
    writes = [
        pltpu.make_async_copy(sums.at[p], target, sems.at[k])
        for k, (p, target) in enumerate(writes)
    ]
    for copy in writes:
        copy.start()
    for copy in writes:
        copy.wait()


def add_parts(gots, masks, outs, places, sizes=(), kept=None):
    n = len(places)
    ins = [*gots, *masks]
    messages = [jax.ShapeDtypeStruct((coded_rows(max(sizes, default=0)), BF), jnp.int16)] * len(sizes)
    in_specs = [VMEM] * len(gots) + [SMEM, VMEM][: len(masks)]
    scratch, aliases = [], {}
    if kept is not None:
        shapes = messages + [jax.ShapeDtypeStruct((kept, SLICE, BF), jnp.float32)]
        out_specs = [VMEM] * len(shapes)
    else:
        shapes = OUTS + messages
        out_specs = [HBM] * 2 + [VMEM] * len(messages)
        scratch = [pltpu.VMEM((n, SLICE, BF), jnp.float32), pltpu.SemaphoreType.DMA((2 * n,))]
        if outs is not None:
            aliases = {len(ins): 0, len(ins) + 1: 1}
            ins += outs
            in_specs += [HBM] * 2
    kernel = functools.partial(
        add_kernel, places, outs is None, sizes, kept is not None, len(gots), len(masks) > 1
    )
    return pl.pallas_call(
        kernel,
        out_shape=shapes,
        in_specs=in_specs,
        out_specs=out_specs,
        scratch_shapes=scratch,
        input_output_aliases=aliases,
        compiler_params=PARAMS,
        cost_estimate=pl.CostEstimate(flops=1 << 20, bytes_accessed=1 << 16, transcendentals=0),
    )(*ins)


def place_kernel(below_places, above_places, block_places, n, first_ref, second_ref, *refs):
    blocks, refs = refs[:n], refs[n + 2 :]
    f_ref, b_ref, sums, sems = refs
    odd = here()[2] == 1
    end = first_ref.shape[0] - 16
    scales = [scales_of(ref[end : end + 16, :]) for ref in (first_ref, second_ref)]
    writes = []

    def write(source, goal):
        kind, block, slot = goal
        target = (f_ref if kind == "f" else b_ref).at[block, slot]
        writes.append(pltpu.make_async_copy(source, target, sems.at[len(writes)]))
        writes[-1].start()

    goals = iter(block_places)
    for ref in blocks:
        for source in [ref] if len(ref.shape) == 2 else [ref.at[k] for k in range(ref.shape[0])]:
            write(source, next(goals))
    k = 0
    for p in range(max(len(below_places), len(above_places))):
        rows = slice(p * SLICE, (p + 1) * SLICE)
        first, second = (
            ref[rows, :].astype(jnp.float32) * scale[p : p + 1]
            for ref, scale in zip((first_ref, second_ref), scales)
        )
        for places, values in ((below_places, (second, first)), (above_places, (first, second))):
            if p < len(places):
                sums[k] = jnp.where(odd, *values)
                write(sums.at[k], places[p])
                k += 1
    for copy in writes:
        copy.wait()


def place_results(first, second, outs, below_places, above_places, blocks=(), block_places=()):
    total = len(below_places) + len(above_places)
    n = 2 + len(blocks)
    return pl.pallas_call(
        functools.partial(place_kernel, below_places, above_places, block_places, len(blocks)),
        out_shape=OUTS,
        in_specs=[VMEM] * n + [HBM] * 2,
        out_specs=[HBM] * 2,
        scratch_shapes=[
            pltpu.VMEM((total, SLICE, BF), jnp.float32),
            pltpu.SemaphoreType.DMA((total + len(block_places),)),
        ],
        input_output_aliases={n: 0, n + 1: 1},
        compiler_params=PARAMS,
        cost_estimate=pl.CostEstimate(flops=1 << 20, bytes_accessed=1 << 16, transcendentals=0),
    )(first, second, *blocks, *outs)


def swap(value):
    return lax.ppermute(value, "occ", [(o, o ^ 1) for o in range(2 * CHIPS)])


def chips_on(value, by):
    pairs = [
        (2 * y + core, 2 * ((y + by) % CHIPS) + core) for y in range(CHIPS) for core in range(2)
    ]
    return lax.ppermute(value, "occ", pairs)


def across(value):
    groups = [[2 * y + core for y in range(CHIPS)] for core in range(2)]
    return lax.all_to_all(value, "occ", 0, 0, axis_index_groups=groups)


def to_chips(parts):
    return [parts[0]] + [chips_on(parts[d], AWAY[d]) for d in range(1, CHIPS)]


def pairwise(first, second):
    size = lax.axis_size("space")
    done = []
    for value, start in ((first, 1), (second, 0)):
        pairs = [(i, i + 1) for i in range(start, size - 1, 2)]
        pairs += [(j, i) for i, j in pairs]
        done.append(lax.ppermute(value, "space", sorted(pairs)))
    return done


def on_device(own, mask):
    own_sib = swap(own)
    first, second = pairwise(*first_factors(own))
    mine = {"own": own, "sib": own_sib}
    blocks = {k: ([("own", k)], [("sib", k)]) for k in range(3)}
    coded0, first2, second2 = pair_products(
        [(0, 1), (0, 2), (1, 2)], blocks, mine, together=True, mask=mask
    )
    first2, second2 = pairwise(first2, second2)
    got0 = [across(coded0)]
    first, second, got0 = lax.optimization_barrier((first, second, got0))
    low_a, low_b, high, other = arrived(first, second)
    low_as, low_bs, high_sib = swap((low_a, low_b, other))
    blocks["L"] = [("low_a", 0), ("low_b", 0)], [("low_as", 0), ("low_bs", 0)]
    blocks["H"] = [("high", 0)], [("high_sib", 0)]
    near, _ = lax.optimization_barrier((own_sib, low_a))
    coded1 = pair_products(
        [("L", 0), ("L", 1), ("L", 2), (0, "H"), (1, "H"), ("L", "H")],
        blocks,
        {"own": own, "sib": bring(near)}
        | {"low_a": low_a, "low_b": low_b, "low_as": low_as, "low_bs": low_bs}
        | {"high": high, "high_sib": high_sib},
    )
    got1 = to_chips(coded1)
    outs = add_parts(
        got0,
        [mask],
        None,
        [
            ((0, 0, 0), [("f", 0, 0), ("b", 1, 0)]),
            ((0, 0, 1), [("f", 0, 1), ("b", 2, 1)]),
            ((0, 1, 0), [("f", 1, 0), ("b", 2, 0)]),
        ],
    )
    near, _ = lax.optimization_barrier((own_sib, coded1[0]))
    near = bring(near)
    first2, second2, _, outs, near = lax.optimization_barrier((first2, second2, coded1[0], outs, near))
    blocks["H2"] = [("high2", 0)], [("high2", 1)]
    blocks["L2"] = [("low2", 0)], [("low2", 1)]
    late = {"own": own, "sib": near, "first": first2, "second": second2}
    *_, mine_half, other_half, lines = pair_products(
        [("L2", 2)], blocks, late, halved=("L2",), late=True
    )
    other_half = swap(other_half)
    *coded2, _ = pair_products([(0, "H2"), (1, "H2")], blocks, late, late=True)
    coded2 = whole(coded2, mine_half, other_half)
    got2 = to_chips(coded2)
    *outs, up1, down1 = add_parts(
        got1,
        [mask, lines],
        outs,
        [
            ((1, 2, 0), [("b", 0, 0), ("m", 1, 0)]),
            ((1, 2, 1), [("b", 1, 1), ("m", 1, 1)]),
            ((1, 2, 2), [("b", 2, 2), ("m", 1, 2)]),
            ((0, 0, 2), [("f", 0, 2), ("m", 0, 0)]),
            ((0, 1, 1), [("f", 1, 1), ("m", 0, 1)]),
            ((1, 2, 3), [("m", 0, 2), ("m", 1, 3)]),
        ],
        (3, 4),
    )
    first3, second3 = pairwise(up1, down1)
    up2, down2, kept = add_parts(
        got2,
        [mask, lines],
        None,
        [
            ((0, 0, 3), [("kept", 0), ("m", 0, 0)]),
            ((0, 1, 2), [("kept", 1), ("m", 0, 1)]),
            ((1, 1, 3), [("kept", 2), ("m", 1, 0)]),
        ],
        (2, 1),
        kept=3,
    )
    first4, second4 = pairwise(up2, down2)
    outs = place_results(
        first3,
        second3,
        outs,
        [("b", 0, 2), ("b", 0, 1), ("b", 0, 3)],
        [("f", 2, 0), ("f", 2, 1), ("f", 2, 2), ("f", 2, 3)],
        [kept],
        [("f", 0, 3), ("f", 1, 2), ("b", 2, 3)],
    )
    forward, backward = place_results(
        first4, second4, outs, [("b", 1, 3), ("b", 1, 2)], [("f", 1, 3)]
    )
    return jnp.swapaxes(forward, 2, 3), backward


def solution(mesh):
    in_specs = (P("space", None, "occ"), P("space", None))
    out_specs = (P("space", None, None, "occ"), P("space", None, "occ", None))
    return jax.shard_map(
        on_device, mesh=mesh, in_specs=in_specs, out_specs=out_specs, check_vma=False
    )
```
